32 devices in a mesh: groups: 2 (over y), site: 4 (over z), sample: 4 (over x, core).
Axes of the slice: x: 2, y: 2, z: 4, core: 2. Of those that a mesh axis runs over, the one named last changes fastest.
Arguments:
- site_tensor: bfloat16 [8, 2048, 2, 2048], P(('groups', 'site'), None, None, 'sample'), parts along dimension 0, may hold values from -0.25 to 0.25
- fronts_in: bfloat16 [3072, 2048], P(('groups', 'sample')), parts along dimension 0
- outcomes: int32 [8, 1536], P(('groups', 'site'), 'sample'), parts along dimension 0, may hold values from 0 to 1
- charges: int32 [10, 16], P('groups'), parts along dimension 0, may hold values from 0 to 3
Outputs:
- fronts_out: bfloat16 [8, 1536, 2048], P(('groups', 'site'), 'sample'), parts along dimension 0
- log_steps: float32 [8, 1536], P(('groups', 'site'), 'sample'), parts along dimension 0
The draws below stay inside these ranges and needn't reach their ends.
There are 2 independent parts, one for each index of `groups`. The reference program is written for one: setup_inputs(seed, part) draws one part's arguments, and reference() takes and returns one part's arrays. A program takes and returns all parts, laid end to end along the dimension named above; each array names one. Nothing has to cross between parts.
All inputs are finite; a program needn't handle non-finite values.
Results may differ from the reference program's by a relative error of at most 0.012.
Values may be sent and summed in bfloat16 or wider, within the bound.
A program may use at most 128 MiB of HBM per device.

```python
import jax
import jax.numpy as jnp
from jax import lax

BOND = 2048
BLOCK = 128
CHARGES = 4
PHYS = 2
NB = 16
SITES = 4
ROWS = 1536


def draw_fronts_in(key, part):
    values = jax.random.normal(jax.random.fold_in(key, 11), (ROWS, BOND), jnp.float32)
    return jnp.clip(values, -8.0, 8.0).astype(jnp.bfloat16)


def plant(result, key, least, largest):
    longest = result.shape.index(max(result.shape))
    spots = []
    for shift in (0, 1):
        where = [jax.random.randint(jax.random.fold_in(key, axis), (), 0, length) for axis, length in enumerate(result.shape)]
        where[longest] = (where[longest] + shift) % result.shape[longest]
        spots.append(tuple(where))
    return result.at[spots[0]].set(least).at[spots[1]].set(largest)


def block_scale(rng, shape, cuts, smallest, largest):
    level, own = 1.0, jax.random.fold_in(rng, 6)
    for position, blocks in cuts:
        heights = jnp.exp(jax.random.uniform(jax.random.fold_in(own, position), (blocks,), jnp.float32, smallest / len(cuts), largest / len(cuts)))
        level = level * jnp.repeat(heights, shape[position] // blocks).reshape([-1 if axis == position else 1 for axis in range(len(shape))])
    return level


def noise(own_key, shape, width, bound, pieces=(), kind=jnp.bfloat16):
    entries = jax.random.normal(own_key, shape, jnp.float32) * width
    if len(pieces) > 0:
        entries = block_scale(own_key, shape, pieces, -0.22, 0.18) * entries
    return jnp.clip(entries, min=-bound, max=bound).astype(kind)


def setup_inputs(seed: int = 0, part: int = 0) -> dict:
    streams_of = jax.random.split(jax.random.key(seed), 5)
    part_splits = jax.random.split(jax.random.fold_in(streams_of[4], part), 5)
    site_tensor = noise(part_splits[0], (SITES, BOND, PHYS, BOND), (BOND // 4) ** -0.5, 0.25, ((0, 4), (3, 4)))
    fronts_in = draw_fronts_in(jax.random.fold_in(jax.random.fold_in(streams_of[4], part), 71), part)
    outcomes = plant(jax.random.randint(part_splits[2], (SITES, ROWS), 0, 2), jax.random.fold_in(part_splits[2], 1), 0, 1).astype(jnp.int32)
    charges = plant(jax.random.randint(part_splits[3], (SITES + 1, NB), 0, CHARGES), jax.random.fold_in(part_splits[3], 1), 0, CHARGES - 1).astype(jnp.int32)
    return dict(site_tensor=site_tensor, fronts_in=fronts_in, outcomes=outcomes, charges=charges)


epsilon = 1e-06

def block_mask(left_charge, right_charge):
    phases = jnp.arange(2, dtype=jnp.int32)
    return right_charge[None, None, :] == (left_charge[:, None, None] + phases[None, :, None]) % CHARGES

def reference(site_tensor, fronts_in, outcomes, charges):

    def one_site(front_rows, site_idx):
        tensor = lax.dynamic_index_in_dim(site_tensor, site_idx, 0, keepdims=False)
        left_charge = lax.dynamic_index_in_dim(charges, site_idx, 0, keepdims=False)
        right_charge = lax.dynamic_index_in_dim(charges, site_idx + 1, 0, keepdims=False)
        allowed = block_mask(left_charge, right_charge).astype(tensor.dtype)
        masked = (tensor.reshape(NB, BLOCK, 2, NB, BLOCK) * allowed[:, None, :, :, None]).reshape(BOND, 2 * BOND)
        products = jnp.dot(front_rows, masked, preferred_element_type=jnp.float32).reshape(ROWS, 2, BOND)
        picks = lax.dynamic_index_in_dim(outcomes, site_idx, 0, keepdims=False)
        chosen = jnp.where(picks[:, None] == 1, products[:, 1], products[:, 0])
        row_norm = jnp.sqrt(lax.optimization_barrier(jnp.mean(chosen * chosen, axis=1)) + epsilon)
        new_front = (chosen / row_norm[:, None]).astype(jnp.bfloat16)
        return (new_front, (new_front, jnp.log(row_norm)))
    final_front, outputs = lax.scan(one_site, fronts_in, jnp.arange(SITES, dtype=jnp.int32))
    return (outputs[0], outputs[1])
```

```python
import functools

import jax
import jax.numpy as jnp
from jax import lax
from jax.experimental import pallas as pl
from jax.experimental.pallas import tpu as pltpu
from jax.sharding import PartitionSpec as P

BLOCK = 128
CHARGES = 4
PHYS = 2
LANES = 128
SUB = 16
MESH = pl.DeviceIdType.MESH

epsilon = 1e-06


def chain_kernel(
    chips, sites, parts_k, micro, wc_ref, mask_ref, fronts_ref, picks_ref,
    out_ref, log_ref,
    wg, wf, held, lhs, chosen,
    x_send, x_recv, s_send, s_recv, z_send, z_recv,
):
    site = lax.axis_index("site")
    me = lax.axis_index("sample")
    chip, core = me // 2, lax.rem(me, 2)
    sibling = chip * 2 + (1 - core)
    bond, cols = wc_ref.shape
    rows = fronts_ref.shape[0]
    depth = bond // parts_k
    steps = rows // micro
    width = cols * 2 * chips

    def chip_ahead(d):
        return lax.rem(chip + d, chips)

    def chip_behind(d):
        return lax.rem(chip + chips - d, chips)

    barrier = pltpu.get_barrier_semaphore()
    pl.semaphore_signal(barrier, inc=1, device_id={"sample": sibling}, device_id_type=MESH)
    for d in range(1, chips):
        pl.semaphore_signal(
            barrier, inc=1, device_id={"sample": chip_ahead(d) * 2 + core}, device_id_type=MESH
        )

    @pl.when(site > 0)
    def _():
        pl.semaphore_signal(barrier, inc=1, device_id={"site": site - 1}, device_id_type=MESH)

    @pl.when(site < sites - 1)
    def _():
        pl.semaphore_signal(barrier, inc=1, device_id={"site": site + 1}, device_id_type=MESH)

    ends = jnp.where(site > 0, 1, 0) + jnp.where(site < sites - 1, 1, 0)
    pl.semaphore_wait(barrier, chips + ends)

    def x_copy(d, c):
        span = pl.ds(c * depth, depth)
        return pltpu.make_async_remote_copy(
            src_ref=wc_ref.at[span, :],
            dst_ref=wg.at[me, span, :],
            send_sem=x_send.at[d - 1, c],
            recv_sem=x_recv.at[d - 1, c],
            device_id={"sample": chip_ahead(d) * 2 + core},
            device_id_type=MESH,
        )

    def sib_copy(d, c):
        span = pl.ds(c * depth, depth)
        owner = chip_behind(d) * 2 + core
        src = wc_ref.at[span, :] if d == 0 else wg.at[owner, span, :]
        return pltpu.make_async_remote_copy(
            src_ref=src,
            dst_ref=wg.at[owner, span, :],
            send_sem=s_send.at[d, c],
            recv_sem=s_recv.at[d, c],
            device_id={"sample": sibling},
            device_id_type=MESH,
        )

    def x_arrival(d, c):
        span = pl.ds(c * depth, depth)
        slot = wg.at[chip_behind(d) * 2 + core, span, :]
        return pltpu.make_async_remote_copy(
            src_ref=slot, dst_ref=slot,
            send_sem=x_send.at[d - 1, c], recv_sem=x_recv.at[d - 1, c],
            device_id={"sample": chip_ahead(d) * 2 + core}, device_id_type=MESH,
        )

    def sib_arrival(d, c):
        span = pl.ds(c * depth, depth)
        slot = wg.at[chip_behind(d) * 2 + (1 - core), span, :]
        return pltpu.make_async_remote_copy(
            src_ref=slot, dst_ref=slot,
            send_sem=s_send.at[d, c], recv_sem=s_recv.at[d, c],
            device_id={"sample": sibling}, device_id_type=MESH,
        )

    def z_copy(b):
        span = pl.ds(pl.multiple_of(b * micro, SUB), micro)
        return pltpu.make_async_remote_copy(
            src_ref=out_ref.at[span, :],
            dst_ref=held.at[span, :],
            send_sem=z_send.at[b],
            recv_sem=z_recv.at[b],
            device_id={"site": jnp.minimum(site + 1, sites - 1)},
            device_id_type=MESH,
        )

    def expand(src, owner, first, last):
        def body(i, carry):
            for p in range(PHYS):
                allowed = mask_ref[owner, i, p]
                for u in range(BLOCK // SUB):
                    at = pl.multiple_of(i * BLOCK + u * SUB, SUB)
                    wf[owner, pl.ds(p * bond + at, SUB), :] = src[pl.ds(at, SUB), :] * allowed
            return carry

        lax.fori_loop(first, last, body, 0)

    for c in range(parts_k):
        for d in range(1, chips):
            x_copy(d, c).start()
    for c in range(parts_k):
        sib_copy(0, c).start()

    @pl.when(site == 0)
    def _():
        held[...] = fronts_ref[...]

    per = depth // BLOCK
    expand(wc_ref, me, 0, bond // BLOCK)
    for c in range(parts_k):
        sib_arrival(0, c).wait_recv()
        expand(wg.at[sibling], sibling, c * per, (c + 1) * per)
    for c in range(parts_k):
        for d in range(1, chips):
            x_arrival(d, c).wait_recv()
            sib_copy(d, c).start()
            mine = chip_behind(d) * 2 + core
            expand(wg.at[mine], mine, c * per, (c + 1) * per)
        for d in range(1, chips):
            sib_arrival(d, c).wait_recv()
            theirs = chip_behind(d) * 2 + (1 - core)
            expand(wg.at[theirs], theirs, c * per, (c + 1) * per)

    def step(b, carry):
        @pl.when(site > 0)
        def _():
            z_copy(b).wait_recv()

        at = pl.multiple_of(b * micro, SUB)
        span = pl.ds(at, micro)
        picks = picks_ref[span, :]
        for k in range(bond // LANES):
            front = held[span, k * LANES : (k + 1) * LANES]
            second = front * picks
            lhs[:, k * LANES : (k + 1) * LANES] = front - second
            lhs[:, bond + k * LANES : bond + (k + 1) * LANES] = second

        def tile(o, total):
            part = jnp.dot(lhs[...], wf[o], preferred_element_type=jnp.float32)
            chosen[o] = part
            return total + jnp.sum(part * part, axis=1, keepdims=True)

        total = lax.fori_loop(0, 2 * chips, tile, jnp.zeros((micro, 1), jnp.float32))
        norm = jnp.sqrt(total * (1.0 / width) + epsilon)
        log_ref[span, :] = jnp.log(norm)
        scale = 1.0 / norm
        for o in range(2 * chips):
            out_ref[span, o * cols : (o + 1) * cols] = (chosen[o] * scale).astype(jnp.bfloat16)

        @pl.when(site < sites - 1)
        def _():
            z_copy(b).start()

        return carry

    lax.fori_loop(0, steps, step, 0)

    for c in range(parts_k):
        for d in range(1, chips):
            x_copy(d, c).wait_send()
        for d in range(chips):
            sib_copy(d, c).wait_send()

    @pl.when(site < sites - 1)
    def _():
        def drain(b, carry):
            z_copy(b).wait_send()
            return carry

        lax.fori_loop(0, steps, drain, 0)


def micro_rows(rows):
    best = rows
    for count in range(1, rows // SUB + 1):
        if rows % count == 0 and (rows // count) % SUB == 0:
            best = rows // count
            if count >= 8:
                break
    return best


def per_device(site_tensor, fronts_in, outcomes, charges):
    sites = lax.axis_size("site")
    samples = lax.axis_size("sample")
    site = lax.axis_index("site")
    me = lax.axis_index("sample")
    chips = samples // 2
    _, bond, _, cols = site_tensor.shape
    rows = fronts_in.shape[0]
    blocks = bond // BLOCK
    left = lax.dynamic_index_in_dim(charges, site, 0, keepdims=False)
    right = lax.dynamic_index_in_dim(charges, site + 1, 0, keepdims=False)
    phases = jnp.arange(PHYS, dtype=jnp.int32)
    allowed = right[None, None, :] == (left[:, None, None] + phases[None, :, None]) % CHARGES

    own = lax.dynamic_slice_in_dim(allowed, me * (cols // BLOCK), cols // BLOCK, 2)
    own = jnp.repeat(jnp.repeat(own, BLOCK, axis=2), BLOCK, axis=0)
    tensor = site_tensor[0]
    zero = jnp.zeros((), tensor.dtype)
    merged = jnp.where(
        own[:, 0], tensor[:, 0, :], jnp.where(own[:, 1], tensor[:, 1, :], zero)
    )

    mask = jnp.repeat(allowed, BLOCK, axis=2).reshape(blocks, PHYS, samples, cols)
    mask = mask.transpose(2, 0, 1, 3)[:, :, :, None, :].astype(jnp.bfloat16)
    mask = jnp.broadcast_to(mask, (samples, blocks, PHYS, SUB, cols))
    picks = jnp.broadcast_to(outcomes[0][:, None], (rows, LANES)).astype(jnp.bfloat16)

    micro = micro_rows(rows)
    parts_k = 4
    steps = rows // micro
    vmem = pl.BlockSpec(memory_space=pltpu.VMEM)
    fronts, logs = pl.pallas_call(
        functools.partial(chain_kernel, chips, sites, parts_k, micro),
        out_shape=(
            jax.ShapeDtypeStruct((rows, bond), jnp.bfloat16),
            jax.ShapeDtypeStruct((rows, 1), jnp.float32),
        ),
        in_specs=[vmem] * 4,
        out_specs=(vmem, vmem),
        scratch_shapes=[
            pltpu.VMEM((samples, bond, cols), jnp.bfloat16),
            pltpu.VMEM((samples, PHYS * bond, cols), jnp.bfloat16),
            pltpu.VMEM((rows, bond), jnp.bfloat16),
            pltpu.VMEM((micro, PHYS * bond), jnp.bfloat16),
            pltpu.VMEM((samples, micro, cols), jnp.float32),
            pltpu.SemaphoreType.DMA((max(chips - 1, 1), parts_k)),
            pltpu.SemaphoreType.DMA((max(chips - 1, 1), parts_k)),
            pltpu.SemaphoreType.DMA((chips, parts_k)),
            pltpu.SemaphoreType.DMA((chips, parts_k)),
            pltpu.SemaphoreType.DMA((steps,)),
            pltpu.SemaphoreType.DMA((steps,)),
        ],
        compiler_params=pltpu.CompilerParams(
            collective_id=0, has_side_effects=True, vmem_limit_bytes=56 * 2**20
        ),
        cost_estimate=pl.CostEstimate(
            flops=4 * rows * bond * bond, bytes_accessed=8 * bond * bond, transcendentals=rows
        ),
    )(merged, mask, fronts_in, picks)
    return fronts[None], logs.reshape(1, rows)


def solution(mesh):
    in_specs = (
        P(("groups", "site"), None, None, "sample"),
        P(("groups", "sample"), None),
        P(("groups", "site"), "sample"),
        P("groups", None),
    )
    out_specs = (P(("groups", "site"), "sample", None), P(("groups", "site"), "sample"))
    return jax.shard_map(
        per_device, mesh=mesh, in_specs=in_specs, out_specs=out_specs, check_vma=False
    )
```

```python
import functools

import jax
import jax.numpy as jnp
from jax import lax
from jax.experimental import pallas as pl
from jax.experimental.pallas import tpu as pltpu
from jax.sharding import PartitionSpec as P

BLOCK = 128
CHARGES = 4
PHYS = 2
LANES = 128
SUB = 16
MESH = pl.DeviceIdType.MESH

epsilon = 1e-06


def chain_kernel(
    chips, sites, micro, tensor_ref, mask_ref, fronts_ref, picks_ref,
    out_ref, log_ref,
    wf, full, lhs, ybuf, gath, marks, columns, logs,
    x_send, x_recv, s_send, s_recv, z_send, z_recv, a_send, a_recv, p_send, p_recv,
):
    samples = 2 * chips
    site = lax.axis_index("site")
    me = lax.axis_index("sample")
    chip, core = me // 2, lax.rem(me, 2)
    sibling = chip * 2 + (1 - core)
    _, bond, cols = tensor_ref.shape
    rows = fronts_ref.shape[0]
    steps = rows // micro

    def ahead(d):
        return lax.rem(chip + d, chips) * 2 + core

    def behind(d, which):
        return lax.rem(chip + chips - d, chips) * 2 + which

    barrier = pltpu.get_barrier_semaphore()
    for e in range(1, samples):
        pl.semaphore_signal(
            barrier, inc=1, device_id={"sample": lax.rem(me + e, samples)}, device_id_type=MESH
        )

    @pl.when(site > 0)
    def _():
        pl.semaphore_signal(barrier, inc=1, device_id={"site": site - 1}, device_id_type=MESH)

    @pl.when(site < sites - 1)
    def _():
        pl.semaphore_signal(barrier, inc=1, device_id={"site": site + 1}, device_id_type=MESH)

    ends = jnp.where(site > 0, 1, 0) + jnp.where(site < sites - 1, 1, 0)
    pl.semaphore_wait(barrier, samples - 1 + ends)

    def remote(src, dst, sent, got, target):
        return pltpu.make_async_remote_copy(
            src_ref=src, dst_ref=dst, send_sem=sent, recv_sem=got,
            device_id=target, device_id_type=MESH,
        )

    def by_rows(owner, b):
        return full.at[:, b, pl.ds(pl.multiple_of(owner * micro, SUB), micro), :]

    def by_columns(owner, b):
        return full.at[owner, b]

    def both(act):
        @pl.when(site == 0)
        def _():
            act(by_rows)

        @pl.when(site > 0)
        def _():
            act(by_columns)

    def x_copy(block, owner, d, b):
        part = block(owner, b)
        return remote(
            part, part, x_send.at[d - 1, b], x_recv.at[d - 1, b], {"sample": ahead(d)}
        )

    def s_copy(block, owner, d, b):
        part = block(owner, b)
        return remote(part, part, s_send.at[d, b], s_recv.at[d, b], {"sample": sibling})

    def z_copy(b):
        return remote(
            ybuf.at[b], full.at[me, b], z_send.at[b], z_recv.at[b],
            {"site": jnp.minimum(site + 1, sites - 1)},
        )

    def a_copy(e, b):
        target = lax.rem(me + e, samples)
        return remote(
            ybuf.at[b, pl.ds(pl.multiple_of(target * micro, SUB), micro), :],
            gath.at[me, b], a_send.at[e - 1, b], a_recv.at[e - 1, b], {"sample": target},
        )

    def a_arrival(e, b):
        source = lax.rem(me + samples - e, samples)
        return remote(
            gath.at[source, b], gath.at[source, b],
            a_send.at[e - 1, b], a_recv.at[e - 1, b], {"sample": source},
        )

    def p_copy(e):
        target = lax.rem(me + e, samples)
        return remote(
            picks_ref, marks.at[me], p_send.at[e - 1], p_recv.at[e - 1], {"sample": target}
        )

    def p_arrival(e):
        source = lax.rem(me + samples - e, samples)
        return remote(
            marks.at[source], marks.at[source],
            p_send.at[e - 1], p_recv.at[e - 1], {"sample": source},
        )

    def launch(b):
        def act(block):
            for d in range(1, chips):
                x_copy(block, me, d, b).start()
            s_copy(block, me, 0, b).start()

        both(act)

    for e in range(1, samples):
        p_copy(e).start()

    @pl.when(site == 0)
    def _():
        for b in range(steps):
            for o in range(samples):
                full[o, b, pl.ds(pl.multiple_of(me * micro, SUB), micro), :] = fronts_ref[
                    b * micro : (b + 1) * micro, o * cols : (o + 1) * cols
                ]
        launch(0)

    def expand(i, carry):
        for p in range(PHYS):
            allowed = mask_ref[i, p]
            for u in range(BLOCK // SUB):
                at = pl.multiple_of(i * BLOCK + u * SUB, SUB)
                wf[pl.ds(p * bond + at, SUB), :] = tensor_ref[p, pl.ds(at, SUB), :] * allowed
        return carry

    lax.fori_loop(0, bond // BLOCK, expand, 0)

    marks[me] = picks_ref[...]
    for e in range(1, samples):
        p_arrival(e).wait_recv()
    for o in range(samples):
        for j in range(rows // LANES):
            line = marks[o, 0:1, j * LANES : (j + 1) * LANES]
            square = jnp.broadcast_to(line, (LANES, LANES)).T
            columns[o * rows + j * LANES : o * rows + (j + 1) * LANES, :] = square.astype(
                jnp.bfloat16
            )

    @pl.when(site > 0)
    def _():
        z_copy(0).wait_recv()
        launch(0)

    first = jnp.where(site == 0, 1.0, 0.0)

    def step(b, carry):
        @pl.when(b + 1 < steps)
        def _():
            @pl.when(site > 0)
            def _():
                z_copy(b + 1).wait_recv()

            launch(b + 1)

        def gather(block):
            for d in range(1, chips):
                x_copy(block, behind(d, core), d, b).wait_recv()
                s_copy(block, behind(d, core), d, b).start()
            for d in range(chips):
                s_copy(block, behind(d, 1 - core), d, b).wait_recv()

        both(gather)

        scales = []
        for o in range(samples):
            span = slice(o * micro, (o + 1) * micro)
            picks = columns[pl.ds(pl.multiple_of(o * rows + b * micro, SUB), micro), :]
            total = jnp.zeros((micro, LANES), jnp.float32)
            for c in range(samples):
                for k in range(cols // LANES):
                    at = c * cols + k * LANES
                    front = full[c, b, span, k * LANES : (k + 1) * LANES]
                    wide = front.astype(jnp.float32)
                    total = total + wide * wide
                    second = front * picks
                    lhs[span, at : at + LANES] = front - second
                    lhs[span, bond + at : bond + at + LANES] = second
            mean = jnp.sum(total, axis=1, keepdims=True) * (1.0 / bond)
            inverse = 1.0 / jnp.sqrt(mean + epsilon)
            scales.append(inverse + first * (1.0 - inverse))
        scale = jnp.concatenate(scales, axis=0)
        tile = min(256, cols)
        for t in range(cols // tile):
            part = jnp.dot(
                lhs[...], wf[:, t * tile : (t + 1) * tile], preferred_element_type=jnp.float32
            )
            ybuf[b, :, t * tile : (t + 1) * tile] = (part * scale).astype(jnp.bfloat16)

        @pl.when(site < sites - 1)
        def _():
            z_copy(b).start()

        @pl.when(site == sites - 1)
        def _():
            for e in range(1, samples):
                a_copy(e, b).start()

        return carry

    lax.fori_loop(0, steps, step, 0)

    @pl.when(site < sites - 1)
    def _():
        def spread(b, carry):
            for e in range(1, samples):
                a_copy(e, b).start()
            return carry

        lax.fori_loop(0, steps, spread, 0)

    def finish(b, carry):
        gath[me, b] = ybuf[b, pl.ds(pl.multiple_of(me * micro, SUB), micro), :]
        for e in range(1, samples):
            a_arrival(e, b).wait_recv()
        total = jnp.zeros((micro, LANES), jnp.float32)
        for c in range(samples):
            for k in range(cols // LANES):
                wide = gath[c, b, :, k * LANES : (k + 1) * LANES].astype(jnp.float32)
                total = total + wide * wide
        norm = jnp.sqrt(jnp.sum(total, axis=1, keepdims=True) * (1.0 / bond) + epsilon)
        inverse = 1.0 / norm
        span = pl.ds(pl.multiple_of(b * micro, SUB), micro)
        logs[span, :] = jnp.broadcast_to(jnp.log(norm), (micro, LANES))
        for c in range(samples):
            wide = gath[c, b].astype(jnp.float32)
            out_ref[span, c * cols : (c + 1) * cols] = (wide * inverse).astype(jnp.bfloat16)
        return carry

    lax.fori_loop(0, steps, finish, 0)
    for j in range(rows // LANES):
        square = logs[j * LANES : (j + 1) * LANES, :].T
        log_ref[0:1, j * LANES : (j + 1) * LANES] = square[0:1, :]

    for e in range(1, samples):
        p_copy(e).wait_send()

    def drain(b, carry):
        def act(block):
            for d in range(1, chips):
                x_copy(block, me, d, b).wait_send()
            for d in range(chips):
                s_copy(block, behind(d, core), d, b).wait_send()

        both(act)
        for e in range(1, samples):
            a_copy(e, b).wait_send()

        @pl.when(site < sites - 1)
        def _():
            z_copy(b).wait_send()

        return carry

    lax.fori_loop(0, steps, drain, 0)


def micro_rows(rows):
    best = rows
    for count in range(1, rows // SUB + 1):
        if rows % count == 0 and (rows // count) % SUB == 0:
            best = rows // count
            if count >= 8:
                break
    return best


def per_device(site_tensor, fronts_in, outcomes, charges):
    sites = lax.axis_size("site")
    samples = lax.axis_size("sample")
    site = lax.axis_index("site")
    me = lax.axis_index("sample")
    chips = samples // 2
    _, bond, _, cols = site_tensor.shape
    rows = fronts_in.shape[0]
    here = cols // BLOCK
    left = lax.dynamic_index_in_dim(charges, site, 0, keepdims=False)
    right = lax.dynamic_slice(charges, (site + 1, me * here), (1, here))[0]
    phases = jnp.arange(PHYS, dtype=jnp.int32)
    allowed = right[None, None, :] == (left[:, None, None] + phases[None, :, None]) % CHARGES
    mask = jnp.repeat(allowed, BLOCK, axis=2)[:, :, None, :].astype(jnp.bfloat16)
    mask = jnp.broadcast_to(mask, (bond // BLOCK, PHYS, SUB, cols))
    tensor = site_tensor[0].transpose(1, 0, 2)
    picks = jnp.broadcast_to(outcomes.astype(jnp.float32), (8, rows))

    micro = micro_rows(rows)
    steps = rows // micro
    vmem = pl.BlockSpec(memory_space=pltpu.VMEM)
    dma = pltpu.SemaphoreType.DMA
    peers = max(chips - 1, 1)
    fronts, logs = pl.pallas_call(
        functools.partial(chain_kernel, chips, sites, micro),
        out_shape=(
            jax.ShapeDtypeStruct((rows, bond), jnp.bfloat16),
            jax.ShapeDtypeStruct((1, rows), jnp.float32),
        ),
        in_specs=[vmem] * 4,
        out_specs=(vmem, vmem),
        scratch_shapes=[
            pltpu.VMEM((PHYS * bond, cols), jnp.bfloat16),
            pltpu.VMEM((samples, steps, samples * micro, cols), jnp.bfloat16),
            pltpu.VMEM((samples * micro, PHYS * bond), jnp.bfloat16),
            pltpu.VMEM((steps, samples * micro, cols), jnp.bfloat16),
            pltpu.VMEM((samples, steps, micro, cols), jnp.bfloat16),
            pltpu.VMEM((samples, 8, rows), jnp.float32),
            pltpu.VMEM((samples * rows, LANES), jnp.bfloat16),
            pltpu.VMEM((rows, LANES), jnp.float32),
            dma((peers, steps)),
            dma((peers, steps)),
            dma((chips, steps)),
            dma((chips, steps)),
            dma((steps,)),
            dma((steps,)),
            dma((samples - 1, steps)),
            dma((samples - 1, steps)),
            dma((samples - 1,)),
            dma((samples - 1,)),
        ],
        compiler_params=pltpu.CompilerParams(
            collective_id=0, has_side_effects=True, vmem_limit_bytes=56 * 2**20
        ),
        cost_estimate=pl.CostEstimate(
            flops=4 * rows * bond * bond, bytes_accessed=8 * bond * bond, transcendentals=rows
        ),
    )(tensor, mask, fronts_in, picks)
    return fronts[None], logs


def solution(mesh):
    in_specs = (
        P(("groups", "site"), None, None, "sample"),
        P(("groups", "sample"), None),
        P(("groups", "site"), "sample"),
        P("groups", None),
    )
    out_specs = (P(("groups", "site"), "sample", None), P(("groups", "site"), "sample"))
    return jax.shard_map(
        per_device, mesh=mesh, in_specs=in_specs, out_specs=out_specs, check_vma=False
    )
```

```python
import functools

import jax
import jax.numpy as jnp
from jax import lax
from jax.experimental import pallas as pl
from jax.experimental.pallas import tpu as pltpu
from jax.sharding import PartitionSpec as P

BLOCK = 128
CHARGES = 4
PHYS = 2
LANES = 128
SUB = 16
MESH = pl.DeviceIdType.MESH

epsilon = 1e-06


def chain_kernel(
    chips, sites, micro, pieces, tensor_ref, charges_ref, fronts_ref, picks_ref,
    out_ref, log_ref,
    wf, wx, merged, landed, full, lhs, ybuf, gath, marks, columns, logs,
    x_send, x_recv, s_send, s_recv, z_send, z_recv, a_send, a_recv, p_send, p_recv,
    w_send, w_recv,
):
    samples = 2 * chips
    site = lax.axis_index("site")
    me = lax.axis_index("sample")
    chip, core = me // 2, lax.rem(me, 2)
    sibling = chip * 2 + (1 - core)
    _, bond, cols = tensor_ref.shape
    rows = fronts_ref.shape[0]
    steps = rows // micro
    pair = 2 * micro
    depth = bond // pieces
    tail = sites - 1 if sites > 1 else sites
    is_tail, is_body = site == tail, site != tail

    def ahead(d):
        return lax.rem(chip + d, chips) * 2 + core

    def behind(d, which):
        return lax.rem(chip + chips - d, chips) * 2 + which

    barrier = pltpu.get_barrier_semaphore()
    for e in range(1, samples):
        pl.semaphore_signal(
            barrier, inc=1, device_id={"sample": lax.rem(me + e, samples)}, device_id_type=MESH
        )

    @pl.when(site > 0)
    def _():
        pl.semaphore_signal(barrier, inc=1, device_id={"site": site - 1}, device_id_type=MESH)

    @pl.when(site < sites - 1)
    def _():
        pl.semaphore_signal(barrier, inc=1, device_id={"site": site + 1}, device_id_type=MESH)

    ends = jnp.where(site > 0, 1, 0) + jnp.where(site < sites - 1, 1, 0)
    pl.semaphore_wait(barrier, samples - 1 + ends)

    def remote(src, dst, sent, got, target):
        return pltpu.make_async_remote_copy(
            src_ref=src, dst_ref=dst, send_sem=sent, recv_sem=got,
            device_id=target, device_id_type=MESH,
        )

    def by_rows(owner, b, to):
        return full.at[:, b, pl.ds(pl.multiple_of(owner * micro, SUB), micro), :]

    def by_columns(owner, b, to):
        return full.at[owner, b]

    def by_chip(owner, b, to):
        return full.at[owner, b, pl.ds(pl.multiple_of(to * pair, SUB), pair), :]

    def each(act):
        @pl.when(site == 0)
        def _():
            act(by_rows)

        @pl.when((site > 0) & (site < tail))
        def _():
            act(by_columns)

        @pl.when(is_tail)
        def _():
            act(by_chip)

    def x_copy(block, owner, d, b, to):
        part = block(owner, b, to)
        return remote(
            part, part, x_send.at[d - 1, b], x_recv.at[d - 1, b], {"sample": ahead(d)}
        )

    def s_copy(block, owner, d, b):
        part = block(owner, b, chip)
        return remote(part, part, s_send.at[d, b], s_recv.at[d, b], {"sample": sibling})

    def w_copy(d, c):
        span = pl.ds(c * depth, depth)
        return remote(
            merged.at[span, :], landed.at[d - 1, span, :],
            w_send.at[d - 1, c], w_recv.at[d - 1, c], {"sample": ahead(d)},
        )

    def t_rows(d, b, which):
        at = pl.multiple_of(d * pair + which * micro, SUB)
        return pl.ds(at, micro)

    def t_copy(d, b):
        return remote(
            ybuf.at[b, t_rows(d, b, 1 - core), :], gath.at[behind(d, core), b],
            a_send.at[d, b], a_recv.at[d, b], {"sample": sibling},
        )

    def t_arrival(d, b):
        slot = gath.at[behind(d, 1 - core), b]
        return remote(slot, slot, a_send.at[d, b], a_recv.at[d, b], {"sample": sibling})

    def z_copy(b):
        return remote(
            ybuf.at[b], full.at[me, b], z_send.at[b], z_recv.at[b],
            {"site": jnp.minimum(site + 1, sites - 1)},
        )

    def a_copy(e, b):
        target = lax.rem(me + e, samples)
        return remote(
            ybuf.at[b, pl.ds(pl.multiple_of(target * micro, SUB), micro), :],
            gath.at[me, b], a_send.at[e - 1, b], a_recv.at[e - 1, b], {"sample": target},
        )

    def a_arrival(e, b):
        source = lax.rem(me + samples - e, samples)
        return remote(
            gath.at[source, b], gath.at[source, b],
            a_send.at[e - 1, b], a_recv.at[e - 1, b], {"sample": source},
        )

    def p_copy(e):
        target = lax.rem(me + e, samples)
        return remote(
            marks.at[me], marks.at[me], p_send.at[e - 1], p_recv.at[e - 1], {"sample": target}
        )

    def p_arrival(e):
        source = lax.rem(me + samples - e, samples)
        return remote(
            marks.at[source], marks.at[source],
            p_send.at[e - 1], p_recv.at[e - 1], {"sample": source},
        )

    def launch(b):
        def act(block):
            for d in range(1, chips):
                x_copy(block, me, d, b, lax.rem(chip + d, chips)).start()
            s_copy(block, me, 0, b).start()

        each(act)

    marks[me] = jnp.broadcast_to(picks_ref[...].astype(jnp.float32), (8, rows))
    for e in range(1, samples):
        p_copy(e).start()

    @pl.when(site == 0)
    def _():
        for b in range(steps):
            for o in range(samples):
                full[o, b, pl.ds(pl.multiple_of(me * micro, SUB), micro), :] = fronts_ref[
                    b * micro : (b + 1) * micro, o * cols : (o + 1) * cols
                ]
        launch(0)

    def expand(owner, load, save, first, last):
        def body(i, carry):
            left = charges_ref[site, i]
            for j in range(cols // BLOCK):
                right = charges_ref[site + 1, owner * (cols // BLOCK) + j]
                allowed = []
                for p in range(PHYS):
                    fits = jnp.where(right == lax.rem(left + p, CHARGES), 1.0, 0.0)
                    allowed.append(jnp.full((SUB, BLOCK), fits, jnp.float32).astype(jnp.bfloat16))
                lanes = slice(j * BLOCK, (j + 1) * BLOCK)
                for u in range(BLOCK // SUB):
                    at = pl.multiple_of(i * BLOCK + u * SUB, SUB)
                    save(at, lanes, [load(p, at, lanes) * allowed[p] for p in range(PHYS)])
            return carry

        lax.fori_loop(first, last, body, 0)

    def load_own(p, at, lanes):
        return tensor_ref[p, pl.ds(at, SUB), lanes]

    def save_own(at, lanes, values):
        for p in range(PHYS):
            wf[pl.ds(p * bond + at, SUB), lanes] = values[p]

    def save_tail(at, lanes, values):
        save_own(at, lanes, values)
        merged[pl.ds(at, SUB), lanes] = values[0] + values[1]

    per = depth // BLOCK

    @pl.when(is_body)
    def _():
        expand(me, load_own, save_own, 0, bond // BLOCK)

    @pl.when(is_tail)
    def _():
        for c in range(pieces):
            expand(me, load_own, save_tail, c * per, (c + 1) * per)
            for d in range(1, chips):
                w_copy(d, c).start()

    for e in range(1, samples):
        p_arrival(e).wait_recv()
    for o in range(samples):
        for j in range(rows // LANES):
            line = marks[o, 0:1, j * LANES : (j + 1) * LANES]
            square = jnp.broadcast_to(line, (LANES, LANES)).T
            columns[o * rows + j * LANES : o * rows + (j + 1) * LANES, :] = square.astype(
                jnp.bfloat16
            )

    @pl.when(is_tail)
    def _():
        for c in range(pieces):
            for d in range(1, chips):
                w_copy(d, c).wait_recv()

                def load_far(p, at, lanes):
                    return landed[d - 1, pl.ds(at, SUB), lanes]

                def save_far(at, lanes, values):
                    for p in range(PHYS):
                        wx[d - 1, pl.ds(p * bond + at, SUB), lanes] = values[p]

                expand(behind(d, core), load_far, save_far, c * per, (c + 1) * per)

    @pl.when(site > 0)
    def _():
        z_copy(0).wait_recv()
        launch(0)

    first = jnp.where(site == 0, 1.0, 0.0)

    def prepare(b, owners):
        scales = []
        for n, o in enumerate(owners):
            span = slice(n * micro, (n + 1) * micro)
            picks = columns[pl.ds(pl.multiple_of(o * rows + b * micro, SUB), micro), :]
            total = jnp.zeros((micro, LANES), jnp.float32)
            for c in range(samples):
                for k in range(cols // LANES):
                    at = c * cols + k * LANES
                    front = full[
                        c, b, pl.ds(pl.multiple_of(o * micro, SUB), micro),
                        k * LANES : (k + 1) * LANES,
                    ]
                    wide = front.astype(jnp.float32)
                    total = total + wide * wide
                    second = front * picks
                    lhs[span, at : at + LANES] = front - second
                    lhs[span, bond + at : bond + at + LANES] = second
            mean = jnp.sum(total, axis=1, keepdims=True) * (1.0 / bond)
            inverse = 1.0 / jnp.sqrt(mean + epsilon)
            scales.append(inverse + first * (1.0 - inverse))
        return jnp.concatenate(scales, axis=0)

    tile = min(256, cols)

    def finish(b):
        total = jnp.zeros((micro, LANES), jnp.float32)
        for c in range(samples):
            for k in range(cols // LANES):
                wide = gath[c, b, :, k * LANES : (k + 1) * LANES].astype(jnp.float32)
                total = total + wide * wide
        norm = jnp.sqrt(jnp.sum(total, axis=1, keepdims=True) * (1.0 / bond) + epsilon)
        inverse = 1.0 / norm
        span = pl.ds(pl.multiple_of(b * micro, SUB), micro)
        logs[span, :] = jnp.broadcast_to(jnp.log(norm), (micro, LANES))
        for c in range(samples):
            wide = gath[c, b].astype(jnp.float32)
            out_ref[span, c * cols : (c + 1) * cols] = (wide * inverse).astype(jnp.bfloat16)

    def finish_body(b, carry):
        gath[me, b] = ybuf[b, pl.ds(pl.multiple_of(me * micro, SUB), micro), :]
        for e in range(1, samples):
            a_arrival(e, b).wait_recv()
        finish(b)
        return carry

    def finish_tail(b):
        for d in range(chips):
            t_arrival(d, b).wait_recv()
        finish(b)

    def step(b, carry):
        @pl.when(b + 1 < steps)
        def _():
            @pl.when(site > 0)
            def _():
                z_copy(b + 1).wait_recv()

            launch(b + 1)

        def gather(block):
            for d in range(1, chips):
                x_copy(block, behind(d, core), d, b, chip).wait_recv()
                s_copy(block, behind(d, core), d, b).start()
            for d in range(chips):
                s_copy(block, behind(d, 1 - core), d, b).wait_recv()

        each(gather)

        @pl.when(is_body)
        def _():
            scale = prepare(b, range(samples))
            for t in range(cols // tile):
                part = jnp.dot(
                    lhs[...], wf[:, t * tile : (t + 1) * tile],
                    preferred_element_type=jnp.float32,
                )
                ybuf[b, :, t * tile : (t + 1) * tile] = (part * scale).astype(jnp.bfloat16)

            @pl.when(site < sites - 1)
            def _():
                z_copy(b).start()

        @pl.when(is_tail)
        def _():
            scale = prepare(b, [chip * 2, chip * 2 + 1])
            for d in range(chips):
                for t in range(cols // tile):
                    lanes = slice(t * tile, (t + 1) * tile)
                    right = wf[:, lanes] if d == 0 else wx[d - 1, :, lanes]
                    part = jnp.dot(lhs[0:pair, :], right, preferred_element_type=jnp.float32)
                    ybuf[b, d * pair : (d + 1) * pair, lanes] = (part * scale).astype(jnp.bfloat16)
                t_copy(d, b).start()
                gath[behind(d, core), b] = ybuf[b, t_rows(d, b, core), :]

            @pl.when(b > 0)
            def _():
                finish_tail(b - 1)

        return carry

    lax.fori_loop(0, steps, step, 0)

    @pl.when(is_tail)
    def _():
        finish_tail(steps - 1)

    @pl.when(is_body)
    def _():
        def spread(b, carry):
            for e in range(1, samples):
                a_copy(e, b).start()
            return carry

        lax.fori_loop(0, steps, spread, 0)
        lax.fori_loop(0, steps, finish_body, 0)

    for j in range(rows // LANES):
        square = logs[j * LANES : (j + 1) * LANES, :].T
        log_ref[0:1, j * LANES : (j + 1) * LANES] = square[0:1, :]

    for e in range(1, samples):
        p_copy(e).wait_send()

    @pl.when(is_tail)
    def _():
        for c in range(pieces):
            for d in range(1, chips):
                w_copy(d, c).wait_send()

    def drain(b, carry):
        def act(block):
            for d in range(1, chips):
                x_copy(block, me, d, b, lax.rem(chip + d, chips)).wait_send()
            for d in range(chips):
                s_copy(block, behind(d, core), d, b).wait_send()

        each(act)

        @pl.when(is_body)
        def _():
            for e in range(1, samples):
                a_copy(e, b).wait_send()

        @pl.when(is_tail)
        def _():
            for d in range(chips):
                t_copy(d, b).wait_send()

        @pl.when(site < sites - 1)
        def _():
            z_copy(b).wait_send()

        return carry

    lax.fori_loop(0, steps, drain, 0)


def micro_rows(rows):
    best = rows
    for count in range(1, rows // SUB + 1):
        if rows % count == 0 and (rows // count) % SUB == 0:
            best = rows // count
            if count >= 8:
                break
    return best


def per_device(site_tensor, fronts_in, outcomes, charges):
    sites = lax.axis_size("site")
    samples = lax.axis_size("sample")
    chips = samples // 2
    _, bond, _, cols = site_tensor.shape
    rows = fronts_in.shape[0]
    tensor = site_tensor[0].transpose(1, 0, 2)
    pieces = 4

    micro = micro_rows(rows)
    steps = rows // micro
    vmem = pl.BlockSpec(memory_space=pltpu.VMEM)
    dma = pltpu.SemaphoreType.DMA
    peers = max(chips - 1, 1)
    fronts, logs = pl.pallas_call(
        functools.partial(chain_kernel, chips, sites, micro, pieces),
        out_shape=(
            jax.ShapeDtypeStruct((rows, bond), jnp.bfloat16),
            jax.ShapeDtypeStruct((1, rows), jnp.float32),
        ),
        in_specs=[vmem, pl.BlockSpec(memory_space=pltpu.SMEM), vmem, vmem],
        out_specs=(vmem, vmem),
        scratch_shapes=[
            pltpu.VMEM((PHYS * bond, cols), jnp.bfloat16),
            pltpu.VMEM((peers, PHYS * bond, cols), jnp.bfloat16),
            pltpu.VMEM((bond, cols), jnp.bfloat16),
            pltpu.VMEM((peers, bond, cols), jnp.bfloat16),
            pltpu.VMEM((samples, steps, samples * micro, cols), jnp.bfloat16),
            pltpu.VMEM((samples * micro, PHYS * bond), jnp.bfloat16),
            pltpu.VMEM((steps, samples * micro, cols), jnp.bfloat16),
            pltpu.VMEM((samples, steps, micro, cols), jnp.bfloat16),
            pltpu.VMEM((samples, 8, rows), jnp.float32),
            pltpu.VMEM((samples * rows, LANES), jnp.bfloat16),
            pltpu.VMEM((rows, LANES), jnp.float32),
            dma((peers, steps)),
            dma((peers, steps)),
            dma((chips, steps)),
            dma((chips, steps)),
            dma((steps,)),
            dma((steps,)),
            dma((samples - 1, steps)),
            dma((samples - 1, steps)),
            dma((samples - 1,)),
            dma((samples - 1,)),
            dma((peers, pieces)),
            dma((peers, pieces)),
        ],
        compiler_params=pltpu.CompilerParams(
            collective_id=0, has_side_effects=True, vmem_limit_bytes=56 * 2**20
        ),
        cost_estimate=pl.CostEstimate(
            flops=4 * rows * bond * bond, bytes_accessed=8 * bond * bond, transcendentals=rows
        ),
    )(tensor, charges, fronts_in, outcomes)
    return fronts[None], logs


def solution(mesh):
    in_specs = (
        P(("groups", "site"), None, None, "sample"),
        P(("groups", "sample"), None),
        P(("groups", "site"), "sample"),
        P("groups", None),
    )
    out_specs = (P(("groups", "site"), "sample", None), P(("groups", "site"), "sample"))
    return jax.shard_map(
        per_device, mesh=mesh, in_specs=in_specs, out_specs=out_specs, check_vma=False
    )
```

```python
import functools

import jax
import jax.numpy as jnp
from jax import lax
from jax.experimental import pallas as pl
from jax.experimental.pallas import tpu as pltpu
from jax.sharding import PartitionSpec as P

BLOCK = 128
CHARGES = 4
PHYS = 2
LANES = 128
SUB = 16
MESH = pl.DeviceIdType.MESH

epsilon = 1e-06


def chain_kernel(
    chips, sites, micro, pieces, tensor_ref, charges_ref, fronts_ref, picks_ref,
    out_ref, log_ref,
    wf, wx, merged, landed, full, acc, sums, ybuf, gath, marks, columns, logs,
    x_send, x_recv, s_send, s_recv, z_send, z_recv, a_send, a_recv, p_send, p_recv,
    w_send, w_recv, b_send, b_recv,
):
    samples = 2 * chips
    site = lax.axis_index("site")
    me = lax.axis_index("sample")
    chip, core = me // 2, lax.rem(me, 2)
    sibling = chip * 2 + (1 - core)
    _, bond, cols = tensor_ref.shape
    rows = fronts_ref.shape[0]
    steps = rows // micro
    pair = 2 * micro
    depth = bond // pieces
    tail = sites - 1
    is_tail, is_body = site == tail, site != tail

    def ahead(d):
        return lax.rem(chip + d, chips) * 2 + core

    def behind(d, which):
        return lax.rem(chip + chips - d, chips) * 2 + which

    barrier = pltpu.get_barrier_semaphore()
    for e in range(1, samples):
        pl.semaphore_signal(
            barrier, inc=1, device_id={"sample": lax.rem(me + e, samples)}, device_id_type=MESH
        )

    @pl.when(site > 0)
    def _():
        pl.semaphore_signal(barrier, inc=1, device_id={"site": site - 1}, device_id_type=MESH)

    @pl.when(site < sites - 1)
    def _():
        pl.semaphore_signal(barrier, inc=1, device_id={"site": site + 1}, device_id_type=MESH)

    ends = jnp.where(site > 0, 1, 0) + jnp.where(site < sites - 1, 1, 0)
    pl.semaphore_wait(barrier, samples - 1 + ends)

    def remote(src, dst, sent, got, target):
        return pltpu.make_async_remote_copy(
            src_ref=src, dst_ref=dst, send_sem=sent, recv_sem=got,
            device_id=target, device_id_type=MESH,
        )

    def by_rows(owner, b, to):
        return full.at[:, b, pl.ds(pl.multiple_of(owner * micro, SUB), micro), :]

    def by_columns(owner, b, to):
        return full.at[owner, b]

    def by_chip(owner, b, to):
        return full.at[owner, b, pl.ds(pl.multiple_of(to * pair, SUB), pair), :]

    def each(act):
        @pl.when(site == 0)
        def _():
            act(by_rows)

        @pl.when((site > 0) & (site < tail))
        def _():
            act(by_columns)

        @pl.when(is_tail)
        def _():
            act(by_chip)

    def x_copy(block, owner, d, b, to):
        part = block(owner, b, to)
        return remote(
            part, part, x_send.at[d - 1, b], x_recv.at[d - 1, b], {"sample": ahead(d)}
        )

    def s_copy(block, owner, d, b):
        part = block(owner, b, chip)
        return remote(part, part, s_send.at[d, b], s_recv.at[d, b], {"sample": sibling})

    def w_copy(d, c):
        span = pl.ds(c * depth, depth)
        return remote(
            merged.at[span, :], landed.at[d - 1, span, :],
            w_send.at[d - 1, c], w_recv.at[d - 1, c], {"sample": ahead(d)},
        )

    def t_rows(d, b, which):
        at = pl.multiple_of(d * pair + which * micro, SUB)
        return pl.ds(at, micro)

    def t_copy(d, b):
        return remote(
            ybuf.at[b, t_rows(d, b, 1 - core), :], gath.at[behind(d, core), b],
            a_send.at[d, b], a_recv.at[d, b], {"sample": sibling},
        )

    def t_arrival(d, b):
        slot = gath.at[behind(d, 1 - core), b]
        return remote(slot, slot, a_send.at[d, b], a_recv.at[d, b], {"sample": sibling})

    def z_copy(b):
        return remote(
            ybuf.at[b], full.at[me, b], z_send.at[b], z_recv.at[b],
            {"site": jnp.minimum(site + 1, sites - 1)},
        )

    def b_copy(b):
        return remote(
            full.at[:, b, pl.ds(pl.multiple_of(me * micro, SUB), micro), :],
            gath.at[:, b], b_send.at[b], b_recv.at[b],
            {"site": jnp.maximum(site - 1, 0)},
        )

    def p_copy(e):
        target = lax.rem(me + e, samples)
        return remote(
            marks.at[me], marks.at[me], p_send.at[e - 1], p_recv.at[e - 1], {"sample": target}
        )

    def p_arrival(e):
        source = lax.rem(me + samples - e, samples)
        return remote(
            marks.at[source], marks.at[source],
            p_send.at[e - 1], p_recv.at[e - 1], {"sample": source},
        )

    def launch(b):
        def act(block):
            for d in range(1, chips):
                x_copy(block, me, d, b, lax.rem(chip + d, chips)).start()
            s_copy(block, me, 0, b).start()

        each(act)

    marks[me] = jnp.broadcast_to(picks_ref[...].astype(jnp.float32), (8, rows))
    for e in range(1, samples):
        p_copy(e).start()

    @pl.when(site == 0)
    def _():
        for b in range(steps):
            for o in range(samples):
                full[o, b, pl.ds(pl.multiple_of(me * micro, SUB), micro), :] = fronts_ref[
                    b * micro : (b + 1) * micro, o * cols : (o + 1) * cols
                ]
        launch(0)

    def expand(owner, load, save, first, last):
        def body(i, carry):
            left = charges_ref[site, i]
            here = cols // BLOCK
            part, inner = i // here, lax.rem(i, here) * BLOCK
            for j in range(cols // BLOCK):
                right = charges_ref[site + 1, owner * (cols // BLOCK) + j]
                allowed = []
                for p in range(PHYS):
                    fits = jnp.where(right == lax.rem(left + p, CHARGES), 1.0, 0.0)
                    allowed.append(jnp.full((SUB, BLOCK), fits, jnp.float32).astype(jnp.bfloat16))
                lanes = slice(j * BLOCK, (j + 1) * BLOCK)
                for u in range(BLOCK // SUB):
                    at = pl.multiple_of(i * BLOCK + u * SUB, SUB)
                    to = (part, pl.multiple_of(inner + u * SUB, SUB))
                    save(to, at, lanes, [load(p, at, lanes) * allowed[p] for p in range(PHYS)])
            return carry

        lax.fori_loop(first, last, body, 0)

    def load_own(p, at, lanes):
        return tensor_ref[p, pl.ds(at, SUB), lanes]

    def save_own(to, at, lanes, values):
        for p in range(PHYS):
            wf[to[0], pl.ds(p * cols + to[1], SUB), lanes] = values[p]

    def save_tail(to, at, lanes, values):
        save_own(to, at, lanes, values)
        merged[pl.ds(at, SUB), lanes] = values[0] + values[1]

    per = depth // BLOCK

    @pl.when(is_body)
    def _():
        expand(me, load_own, save_own, 0, bond // BLOCK)

    @pl.when(is_tail)
    def _():
        for c in range(pieces):
            expand(me, load_own, save_tail, c * per, (c + 1) * per)
            for d in range(1, chips):
                w_copy(d, c).start()

    for e in range(1, samples):
        p_arrival(e).wait_recv()
    for o in range(samples):
        for j in range(rows // LANES):
            line = marks[o, 0:1, j * LANES : (j + 1) * LANES]
            square = jnp.broadcast_to(line, (LANES, LANES)).T.astype(jnp.bfloat16)
            for q in range(LANES // micro):
                columns[j * (LANES // micro) + q, o * micro : (o + 1) * micro, :] = square[
                    q * micro : (q + 1) * micro, :
                ]

    @pl.when(is_tail)
    def _():
        for c in range(pieces):
            for d in range(1, chips):
                w_copy(d, c).wait_recv()

                def load_far(p, at, lanes):
                    return landed[d - 1, pl.ds(at, SUB), lanes]

                def save_far(to, at, lanes, values):
                    for p in range(PHYS):
                        wx[d - 1, to[0], pl.ds(p * cols + to[1], SUB), lanes] = values[p]

                expand(behind(d, core), load_far, save_far, c * per, (c + 1) * per)

    @pl.when(site > 0)
    def _():
        z_copy(0).wait_recv()
        launch(0)

    first = jnp.where(site == 0, 1.0, 0.0)

    chip_rows = pl.ds(pl.multiple_of(chip * pair, SUB), pair)

    def contract(b, c, start, last):
        if last:
            front, picks, count = full[c, b, chip_rows, :], columns[b, chip_rows, :], pair
        else:
            front, picks, count = full[c, b], columns[b], samples * micro
        second = front * jnp.concatenate([picks] * (cols // LANES), axis=1)
        both = jnp.concatenate([front - second, second], axis=1)
        total = jnp.zeros((count, LANES), jnp.float32)
        for k in range(cols // LANES):
            wide = front[:, k * LANES : (k + 1) * LANES].astype(jnp.float32)
            total = total + wide * wide
        sums[0:count, :] = total if start else sums[0:count, :] + total
        for d in range(chips if last else 1):
            right = wf[c] if d == 0 else wx[d - 1, c]
            part = jnp.dot(both, right, preferred_element_type=jnp.float32)
            acc[d, 0:count, :] = part if start else acc[d, 0:count, :] + part

    def scale_of(count):
        mean = jnp.sum(sums[0:count, :], axis=1, keepdims=True) * (1.0 / bond)
        inverse = 1.0 / jnp.sqrt(mean + epsilon)
        return inverse + first * (1.0 - inverse)

    def finish(b):
        total = jnp.zeros((micro, LANES), jnp.float32)
        for c in range(samples):
            for k in range(cols // LANES):
                wide = gath[c, b, :, k * LANES : (k + 1) * LANES].astype(jnp.float32)
                total = total + wide * wide
        norm = jnp.sqrt(jnp.sum(total, axis=1, keepdims=True) * (1.0 / bond) + epsilon)
        inverse = 1.0 / norm
        span = pl.ds(pl.multiple_of(b * micro, SUB), micro)
        logs[span, :] = jnp.broadcast_to(jnp.log(norm), (micro, LANES))
        for c in range(samples):
            wide = gath[c, b].astype(jnp.float32)
            out_ref[span, c * cols : (c + 1) * cols] = (wide * inverse).astype(jnp.bfloat16)

    def finish_body(b, carry):
        b_copy(b).wait_recv()
        finish(b)
        return carry

    def finish_tail(b):
        for d in range(chips):
            t_arrival(d, b).wait_recv()
        finish(b)

    def early(b, block, last):
        contract(b, me, True, last)
        s_copy(block, sibling, 0, b).wait_recv()
        contract(b, sibling, False, last)

    def late(b, block, last):
        for d in range(1, chips):
            x_copy(block, behind(d, core), d, b, chip).wait_recv()
            s_copy(block, behind(d, core), d, b).start()
            contract(b, behind(d, core), False, last)
            s_copy(block, behind(d, 1 - core), d, b).wait_recv()
            contract(b, behind(d, 1 - core), False, last)

    def step(b, carry):
        @pl.when((site > 0) & (site < tail))
        def _():
            early(b, by_columns, False)

        @pl.when(is_tail)
        def _():
            early(b, by_chip, True)

        @pl.when(b + 1 < steps)
        def _():
            @pl.when(site > 0)
            def _():
                z_copy(b + 1).wait_recv()

            launch(b + 1)

        @pl.when(site == 0)
        def _():
            for d in range(1, chips):
                x_copy(by_rows, behind(d, core), d, b, chip).wait_recv()
                s_copy(by_rows, behind(d, core), d, b).start()
            for d in range(chips):
                s_copy(by_rows, behind(d, 1 - core), d, b).wait_recv()
            for c in range(samples):
                contract(b, c, c == 0, False)

        @pl.when((site > 0) & (site < tail))
        def _():
            late(b, by_columns, False)

        @pl.when(is_tail)
        def _():
            late(b, by_chip, True)

        @pl.when(is_body)
        def _():
            ybuf[b] = (acc[0] * scale_of(samples * micro)).astype(jnp.bfloat16)
            z_copy(b).start()

        @pl.when(is_tail)
        def _():
            scale = scale_of(pair)
            for d in range(chips):
                ybuf[b, d * pair : (d + 1) * pair, :] = (acc[d, 0:pair, :] * scale).astype(
                    jnp.bfloat16
                )
                t_copy(d, b).start()
                gath[behind(d, core), b] = ybuf[b, t_rows(d, b, core), :]

        @pl.when(site > 0)
        def _():
            b_copy(b).start()

        @pl.when(is_tail & (b > 0))
        def _():
            finish_tail(b - 1)

        return carry

    lax.fori_loop(0, steps, step, 0)

    @pl.when(is_tail)
    def _():
        finish_tail(steps - 1)

    @pl.when(is_body)
    def _():
        lax.fori_loop(0, steps, finish_body, 0)

    for j in range(rows // LANES):
        square = logs[j * LANES : (j + 1) * LANES, :].T
        log_ref[0:1, j * LANES : (j + 1) * LANES] = square[0:1, :]

    for e in range(1, samples):
        p_copy(e).wait_send()

    @pl.when(is_tail)
    def _():
        for c in range(pieces):
            for d in range(1, chips):
                w_copy(d, c).wait_send()

    def drain(b, carry):
        def act(block):
            for d in range(1, chips):
                x_copy(block, me, d, b, lax.rem(chip + d, chips)).wait_send()
            for d in range(chips):
                s_copy(block, behind(d, core), d, b).wait_send()

        each(act)

        @pl.when(site > 0)
        def _():
            b_copy(b).wait_send()

        @pl.when(is_tail)
        def _():
            for d in range(chips):
                t_copy(d, b).wait_send()

        @pl.when(site < sites - 1)
        def _():
            z_copy(b).wait_send()

        return carry

    lax.fori_loop(0, steps, drain, 0)


def per_device(site_tensor, fronts_in, outcomes, charges):
    sites = lax.axis_size("site")
    samples = lax.axis_size("sample")
    chips = samples // 2
    _, bond, _, cols = site_tensor.shape
    rows = fronts_in.shape[0]
    tensor = site_tensor[0].transpose(1, 0, 2)
    pieces = 4

    micro = 32
    steps = rows // micro
    vmem = pl.BlockSpec(memory_space=pltpu.VMEM)
    dma = pltpu.SemaphoreType.DMA
    peers = max(chips - 1, 1)
    fronts, logs = pl.pallas_call(
        functools.partial(chain_kernel, chips, sites, micro, pieces),
        out_shape=(
            jax.ShapeDtypeStruct((rows, bond), jnp.bfloat16),
            jax.ShapeDtypeStruct((1, rows), jnp.float32),
        ),
        in_specs=[vmem, pl.BlockSpec(memory_space=pltpu.SMEM), vmem, vmem],
        out_specs=(vmem, vmem),
        scratch_shapes=[
            pltpu.VMEM((samples, PHYS * cols, cols), jnp.bfloat16),
            pltpu.VMEM((peers, samples, PHYS * cols, cols), jnp.bfloat16),
            pltpu.VMEM((bond, cols), jnp.bfloat16),
            pltpu.VMEM((peers, bond, cols), jnp.bfloat16),
            pltpu.VMEM((samples, steps, samples * micro, cols), jnp.bfloat16),
            pltpu.VMEM((chips, samples * micro, cols), jnp.float32),
            pltpu.VMEM((samples * micro, LANES), jnp.float32),
            pltpu.VMEM((steps, samples * micro, cols), jnp.bfloat16),
            pltpu.VMEM((samples, steps, micro, cols), jnp.bfloat16),
            pltpu.VMEM((samples, 8, rows), jnp.float32),
            pltpu.VMEM((steps, samples * micro, LANES), jnp.bfloat16),
            pltpu.VMEM((rows, LANES), jnp.float32),
            dma((peers, steps)),
            dma((peers, steps)),
            dma((chips, steps)),
            dma((chips, steps)),
            dma((steps,)),
            dma((steps,)),
            dma((chips, steps)),
            dma((chips, steps)),
            dma((samples - 1,)),
            dma((samples - 1,)),
            dma((peers, pieces)),
            dma((peers, pieces)),
            dma((steps,)),
            dma((steps,)),
        ],
        compiler_params=pltpu.CompilerParams(
            collective_id=0, has_side_effects=True, vmem_limit_bytes=56 * 2**20
        ),
        cost_estimate=pl.CostEstimate(
            flops=4 * rows * bond * bond, bytes_accessed=8 * bond * bond, transcendentals=rows
        ),
    )(tensor, charges, fronts_in, outcomes)
    return fronts[None], logs


def solution(mesh):
    in_specs = (
        P(("groups", "site"), None, None, "sample"),
        P(("groups", "sample"), None),
        P(("groups", "site"), "sample"),
        P("groups", None),
    )
    out_specs = (P(("groups", "site"), "sample", None), P(("groups", "site"), "sample"))
    return jax.shard_map(
        per_device, mesh=mesh, in_specs=in_specs, out_specs=out_specs, check_vma=False
    )
```

```python
import functools

import jax
import jax.numpy as jnp
from jax import lax
from jax.experimental import pallas as pl
from jax.experimental.pallas import tpu as pltpu
from jax.sharding import PartitionSpec as P

BLOCK = 128
CHARGES = 4
PHYS = 2
LANES = 128
SUB = 16
MESH = pl.DeviceIdType.MESH

epsilon = 1e-06


def chain_kernel(
    chips, sites, micro, pieces, tensor_ref, charges_ref, fronts_ref, picks_ref,
    out_ref, log_ref,
    wf, wx, merged, landed, full, acc, sums, ybuf, gath, marks, columns, logs,
    x_send, x_recv, s_send, s_recv, z_send, z_recv, a_send, a_recv, p_send, p_recv,
    w_send, w_recv, b_send, b_recv,
):
    samples = 2 * chips
    site = lax.axis_index("site")
    me = lax.axis_index("sample")
    chip, core = me // 2, lax.rem(me, 2)
    sibling = chip * 2 + (1 - core)
    _, bond, cols = tensor_ref.shape
    rows = fronts_ref.shape[0]
    steps = rows // micro
    pair = 2 * micro
    depth = bond // pieces
    tail = sites - 1
    is_tail, is_body = site == tail, site != tail

    def ahead(d):
        return lax.rem(chip + d, chips) * 2 + core

    def behind(d, which):
        return lax.rem(chip + chips - d, chips) * 2 + which

    barrier = pltpu.get_barrier_semaphore()
    for e in range(1, samples):
        pl.semaphore_signal(
            barrier, inc=1, device_id={"sample": lax.rem(me + e, samples)}, device_id_type=MESH
        )

    @pl.when(site > 0)
    def _():
        pl.semaphore_signal(barrier, inc=1, device_id={"site": site - 1}, device_id_type=MESH)

    @pl.when(site < sites - 1)
    def _():
        pl.semaphore_signal(barrier, inc=1, device_id={"site": site + 1}, device_id_type=MESH)

    ends = jnp.where(site > 0, 1, 0) + jnp.where(site < sites - 1, 1, 0)
    pl.semaphore_wait(barrier, samples - 1 + ends)

    def remote(src, dst, sent, got, target):
        return pltpu.make_async_remote_copy(
            src_ref=src, dst_ref=dst, send_sem=sent, recv_sem=got,
            device_id=target, device_id_type=MESH,
        )

    def by_rows(owner, b, to):
        return full.at[:, b, pl.ds(pl.multiple_of(owner * micro, SUB), micro), :]

    def by_columns(owner, b, to):
        return full.at[owner, b]

    def by_chip(owner, b, to):
        return full.at[owner, b, pl.ds(pl.multiple_of(to * pair, SUB), pair), :]

    def each(act):
        @pl.when(site == 0)
        def _():
            act(by_rows)

        @pl.when((site > 0) & (site < tail))
        def _():
            act(by_columns)

        @pl.when(is_tail)
        def _():
            act(by_chip)

    def x_copy(block, owner, d, b, to):
        part = block(owner, b, to)
        return remote(
            part, part, x_send.at[d - 1, b], x_recv.at[d - 1, b], {"sample": ahead(d)}
        )

    def s_copy(block, owner, d, b):
        part = block(owner, b, chip)
        return remote(part, part, s_send.at[d, b], s_recv.at[d, b], {"sample": sibling})

    def w_copy(d, c):
        span = pl.ds(c * depth, depth)
        return remote(
            merged.at[span, :], landed.at[d - 1, span, :],
            w_send.at[d - 1, c], w_recv.at[d - 1, c], {"sample": ahead(d)},
        )

    def t_rows(d, b, which):
        at = pl.multiple_of(d * pair + which * micro, SUB)
        return pl.ds(at, micro)

    def t_copy(d, b):
        return remote(
            ybuf.at[b, t_rows(d, b, 1 - core), :], gath.at[behind(d, core), b],
            a_send.at[d, b], a_recv.at[d, b], {"sample": sibling},
        )

    def t_arrival(d, b):
        slot = gath.at[behind(d, 1 - core), b]
        return remote(slot, slot, a_send.at[d, b], a_recv.at[d, b], {"sample": sibling})

    def z_copy(b):
        return remote(
            ybuf.at[b], full.at[me, b], z_send.at[b], z_recv.at[b],
            {"site": jnp.minimum(site + 1, sites - 1)},
        )

    def b_copy(b):
        return remote(
            full.at[:, b, pl.ds(pl.multiple_of(me * micro, SUB), micro), :],
            gath.at[:, b], b_send.at[b], b_recv.at[b],
            {"site": jnp.maximum(site - 1, 0)},
        )

    def p_copy(e):
        target = lax.rem(me + e, samples)
        return remote(
            marks.at[me], marks.at[me], p_send.at[e - 1], p_recv.at[e - 1], {"sample": target}
        )

    def p_arrival(e):
        source = lax.rem(me + samples - e, samples)
        return remote(
            marks.at[source], marks.at[source],
            p_send.at[e - 1], p_recv.at[e - 1], {"sample": source},
        )

    def launch(b):
        def act(block):
            for d in range(1, chips):
                x_copy(block, me, d, b, lax.rem(chip + d, chips)).start()
            s_copy(block, me, 0, b).start()

        each(act)

    marks[me] = jnp.broadcast_to(picks_ref[...].astype(jnp.float32), (8, rows))
    for e in range(1, samples):
        p_copy(e).start()

    @pl.when(site == 0)
    def _():
        for b in range(steps):
            for o in range(samples):
                full[o, b, pl.ds(pl.multiple_of(me * micro, SUB), micro), :] = fronts_ref[
                    b * micro : (b + 1) * micro, o * cols : (o + 1) * cols
                ]
        for b in range(min(2, steps)):
            launch(b)

    def expand(owner, load, save, first, last):
        def body(i, carry):
            left = charges_ref[site, i]
            here = cols // BLOCK
            part, inner = i // here, lax.rem(i, here) * BLOCK
            for j in range(cols // BLOCK):
                right = charges_ref[site + 1, owner * (cols // BLOCK) + j]
                allowed = []
                for p in range(PHYS):
                    fits = jnp.where(right == lax.rem(left + p, CHARGES), 1.0, 0.0)
                    allowed.append(jnp.full((SUB, BLOCK), fits, jnp.float32).astype(jnp.bfloat16))
                lanes = slice(j * BLOCK, (j + 1) * BLOCK)
                for u in range(BLOCK // SUB):
                    at = pl.multiple_of(i * BLOCK + u * SUB, SUB)
                    to = (part, pl.multiple_of(inner + u * SUB, SUB))
                    save(to, at, lanes, [load(p, at, lanes) * allowed[p] for p in range(PHYS)])
            return carry

        lax.fori_loop(first, last, body, 0)

    def load_own(p, at, lanes):
        return tensor_ref[p, pl.ds(at, SUB), lanes]

    def save_own(to, at, lanes, values):
        for p in range(PHYS):
            wf[to[0], pl.ds(p * cols + to[1], SUB), lanes] = values[p]

    def save_tail(to, at, lanes, values):
        save_own(to, at, lanes, values)
        merged[pl.ds(at, SUB), lanes] = values[0] + values[1]

    per = depth // BLOCK

    @pl.when(is_body)
    def _():
        expand(me, load_own, save_own, 0, bond // BLOCK)

    @pl.when(is_tail)
    def _():
        for c in range(pieces):
            expand(me, load_own, save_tail, c * per, (c + 1) * per)
            for d in range(1, chips):
                w_copy(d, c).start()

    for e in range(1, samples):
        p_arrival(e).wait_recv()
    for o in range(samples):
        for j in range(rows // LANES):
            line = marks[o, 0:1, j * LANES : (j + 1) * LANES]
            square = jnp.broadcast_to(line, (LANES, LANES)).T.astype(jnp.bfloat16)
            for q in range(LANES // SUB):
                b, at = divmod(j * LANES + q * SUB, micro)
                columns[b, o * micro + at : o * micro + at + SUB, :] = square[
                    q * SUB : (q + 1) * SUB, :
                ]

    @pl.when(is_tail)
    def _():
        for c in range(pieces):
            for d in range(1, chips):
                w_copy(d, c).wait_recv()

                def load_far(p, at, lanes):
                    return landed[d - 1, pl.ds(at, SUB), lanes]

                def save_far(to, at, lanes, values):
                    for p in range(PHYS):
                        wx[d - 1, to[0], pl.ds(p * cols + to[1], SUB), lanes] = values[p]

                expand(behind(d, core), load_far, save_far, c * per, (c + 1) * per)

    @pl.when(site > 0)
    def _():
        z_copy(0).wait_recv()
        launch(0)

    def forward(b):
        for d in range(1, chips):
            x_copy(by_rows, behind(d, core), d, b, chip).wait_recv()
            s_copy(by_rows, behind(d, core), d, b).start()

    @pl.when(site == 0)
    def _():
        forward(0)

    chip_rows = pl.ds(pl.multiple_of(chip * pair, SUB), pair)

    def contract(b, c, start, last, norms=True):
        if last:
            front, picks, count = full[c, b, chip_rows, :], columns[b, chip_rows, :], pair
        else:
            front, picks, count = full[c, b], columns[b], samples * micro
        second = front * jnp.concatenate([picks] * (cols // LANES), axis=1)
        both = jnp.concatenate([front - second, second], axis=1)
        if norms:
            total = jnp.zeros((count, LANES), jnp.float32)
            for k in range(cols // LANES):
                wide = front[:, k * LANES : (k + 1) * LANES].astype(jnp.float32)
                total = total + wide * wide
            sums[0:count, :] = total if start else sums[0:count, :] + total
        for d in range(chips if last else 1):
            right = wf[c] if d == 0 else wx[d - 1, c]
            part = jnp.dot(both, right, preferred_element_type=jnp.float32)
            acc[d, 0:count, :] = part if start else acc[d, 0:count, :] + part

    def scale_of(count):
        mean = jnp.sum(sums[0:count, :], axis=1, keepdims=True) * (1.0 / bond)
        return 1.0 / jnp.sqrt(mean + epsilon)

    def finish(b):
        total = jnp.zeros((micro, LANES), jnp.float32)
        for c in range(samples):
            for k in range(cols // LANES):
                wide = gath[c, b, :, k * LANES : (k + 1) * LANES].astype(jnp.float32)
                total = total + wide * wide
        norm = jnp.sqrt(jnp.sum(total, axis=1, keepdims=True) * (1.0 / bond) + epsilon)
        inverse = 1.0 / norm
        span = pl.ds(pl.multiple_of(b * micro, SUB), micro)
        logs[span, :] = jnp.broadcast_to(jnp.log(norm), (micro, LANES))
        for c in range(samples):
            wide = gath[c, b].astype(jnp.float32)
            out_ref[span, c * cols : (c + 1) * cols] = (wide * inverse).astype(jnp.bfloat16)

    def finish_body(b, carry):
        b_copy(b).wait_recv()
        finish(b)
        return carry

    def finish_tail(b):
        for d in range(chips):
            t_arrival(d, b).wait_recv()
        finish(b)

    def early(b, block, last):
        contract(b, me, True, last)
        s_copy(block, sibling, 0, b).wait_recv()
        contract(b, sibling, False, last)

    def late(b, block, last):
        for d in range(1, chips):
            x_copy(block, behind(d, core), d, b, chip).wait_recv()
            s_copy(block, behind(d, core), d, b).start()
            contract(b, behind(d, core), False, last)
            s_copy(block, behind(d, 1 - core), d, b).wait_recv()
            if d == chips - 1:
                b_copy(b).start()
            contract(b, behind(d, 1 - core), False, last)

    def step(b, carry):
        @pl.when((site > 0) & (site < tail))
        def _():
            early(b, by_columns, False)

        @pl.when(is_tail)
        def _():
            early(b, by_chip, True)

        @pl.when((site > 0) & (b + 1 < steps))
        def _():
            z_copy(b + 1).wait_recv()
            launch(b + 1)

        @pl.when((site == 0) & (b + 2 < steps))
        def _():
            launch(b + 2)

        @pl.when(site == 0)
        def _():
            for d in range(chips):
                s_copy(by_rows, behind(d, 1 - core), d, b).wait_recv()
            for c in range(samples - 1):
                contract(b, c, c == 0, False, False)

            @pl.when(b + 1 < steps)
            def _():
                forward(b + 1)

            contract(b, samples - 1, False, False, False)
            ybuf[b] = acc[0].astype(jnp.bfloat16)
            z_copy(b).start()

        @pl.when((site > 0) & (site < tail))
        def _():
            late(b, by_columns, False)

        @pl.when(is_tail)
        def _():
            late(b, by_chip, True)

        @pl.when((site > 0) & (site < tail))
        def _():
            ybuf[b] = (acc[0] * scale_of(samples * micro)).astype(jnp.bfloat16)
            z_copy(b).start()

        @pl.when(is_tail)
        def _():
            scale = scale_of(pair)
            for d in range(chips):
                ybuf[b, d * pair : (d + 1) * pair, :] = (acc[d, 0:pair, :] * scale).astype(
                    jnp.bfloat16
                )
                t_copy(d, b).start()
                gath[behind(d, core), b] = ybuf[b, t_rows(d, b, core), :]

        @pl.when(is_tail & (b > 0))
        def _():
            finish_tail(b - 1)

        return carry

    lax.fori_loop(0, steps, step, 0)

    @pl.when(is_tail)
    def _():
        finish_tail(steps - 1)

    @pl.when(is_body)
    def _():
        lax.fori_loop(0, steps, finish_body, 0)

    for j in range(rows // LANES):
        square = logs[j * LANES : (j + 1) * LANES, :].T
        log_ref[0:1, j * LANES : (j + 1) * LANES] = square[0:1, :]

    for e in range(1, samples):
        p_copy(e).wait_send()

    @pl.when(is_tail)
    def _():
        for c in range(pieces):
            for d in range(1, chips):
                w_copy(d, c).wait_send()

    def drain(b, carry):
        def act(block):
            for d in range(1, chips):
                x_copy(block, me, d, b, lax.rem(chip + d, chips)).wait_send()
            for d in range(chips):
                s_copy(block, behind(d, core), d, b).wait_send()

        each(act)

        @pl.when(site > 0)
        def _():
            b_copy(b).wait_send()

        @pl.when(is_tail)
        def _():
            for d in range(chips):
                t_copy(d, b).wait_send()

        @pl.when(site < sites - 1)
        def _():
            z_copy(b).wait_send()

        return carry

    lax.fori_loop(0, steps, drain, 0)


def micro_rows(rows):
    best = rows
    for count in range(1, rows // SUB + 1):
        if rows % count == 0 and (rows // count) % SUB == 0:
            best = rows // count
            if count >= 8:
                break
    return best


def per_device(site_tensor, fronts_in, outcomes, charges):
    sites = lax.axis_size("site")
    samples = lax.axis_size("sample")
    chips = samples // 2
    _, bond, _, cols = site_tensor.shape
    rows = fronts_in.shape[0]
    tensor = site_tensor[0].transpose(1, 0, 2)
    pieces = 4

    micro = micro_rows(rows)
    steps = rows // micro
    vmem = pl.BlockSpec(memory_space=pltpu.VMEM)
    dma = pltpu.SemaphoreType.DMA
    peers = max(chips - 1, 1)
    fronts, logs = pl.pallas_call(
        functools.partial(chain_kernel, chips, sites, micro, pieces),
        out_shape=(
            jax.ShapeDtypeStruct((rows, bond), jnp.bfloat16),
            jax.ShapeDtypeStruct((1, rows), jnp.float32),
        ),
        in_specs=[vmem, pl.BlockSpec(memory_space=pltpu.SMEM), vmem, vmem],
        out_specs=(vmem, vmem),
        scratch_shapes=[
            pltpu.VMEM((samples, PHYS * cols, cols), jnp.bfloat16),
            pltpu.VMEM((peers, samples, PHYS * cols, cols), jnp.bfloat16),
            pltpu.VMEM((bond, cols), jnp.bfloat16),
            pltpu.VMEM((peers, bond, cols), jnp.bfloat16),
            pltpu.VMEM((samples, steps, samples * micro, cols), jnp.bfloat16),
            pltpu.VMEM((chips, samples * micro, cols), jnp.float32),
            pltpu.VMEM((samples * micro, LANES), jnp.float32),
            pltpu.VMEM((steps, samples * micro, cols), jnp.bfloat16),
            pltpu.VMEM((samples, steps, micro, cols), jnp.bfloat16),
            pltpu.VMEM((samples, 8, rows), jnp.float32),
            pltpu.VMEM((steps, samples * micro, LANES), jnp.bfloat16),
            pltpu.VMEM((rows, LANES), jnp.float32),
            dma((peers, steps)),
            dma((peers, steps)),
            dma((chips, steps)),
            dma((chips, steps)),
            dma((steps,)),
            dma((steps,)),
            dma((chips, steps)),
            dma((chips, steps)),
            dma((samples - 1,)),
            dma((samples - 1,)),
            dma((peers, pieces)),
            dma((peers, pieces)),
            dma((steps,)),
            dma((steps,)),
        ],
        compiler_params=pltpu.CompilerParams(
            collective_id=0, has_side_effects=True, vmem_limit_bytes=36 * 2**20
        ),
        cost_estimate=pl.CostEstimate(
            flops=4 * rows * bond * bond, bytes_accessed=8 * bond * bond, transcendentals=rows
        ),
    )(tensor, charges, fronts_in, outcomes)
    return fronts[None], logs


def solution(mesh):
    in_specs = (
        P(("groups", "site"), None, None, "sample"),
        P(("groups", "sample"), None),
        P(("groups", "site"), "sample"),
        P("groups", None),
    )
    out_specs = (P(("groups", "site"), "sample", None), P(("groups", "site"), "sample"))
    return jax.shard_map(
        per_device, mesh=mesh, in_specs=in_specs, out_specs=out_specs, check_vma=False
    )
```

```python
import functools

import jax
import jax.numpy as jnp
from jax import lax
from jax.experimental import pallas as pl
from jax.experimental.pallas import tpu as pltpu
from jax.sharding import PartitionSpec as P

BLOCK = 128
CHARGES = 4
PHYS = 2
LANES = 128
SUB = 16
MESH = pl.DeviceIdType.MESH

epsilon = 1e-06


def chain_kernel(
    chips, sites, micro, pieces, tensor_ref, charges_ref, fronts_ref, picks_ref,
    out_ref, log_ref,
    wf, wx, merged, landed, full, acc, sums, ybuf, gath, marks, columns, logs,
    x_send, x_recv, s_send, s_recv, z_send, z_recv, a_send, a_recv, p_send, p_recv,
    w_send, w_recv, b_send, b_recv,
):
    samples = 2 * chips
    site = lax.axis_index("site")
    me = lax.axis_index("sample")
    chip, core = me // 2, lax.rem(me, 2)
    sibling = chip * 2 + (1 - core)
    _, bond, cols = tensor_ref.shape
    rows = fronts_ref.shape[0]
    steps = rows // micro
    pair = 2 * micro
    depth = bond // pieces
    tail = sites - 1
    is_tail, is_body = site == tail, site != tail

    def ahead(d):
        return lax.rem(chip + d, chips) * 2 + core

    def behind(d, which):
        return lax.rem(chip + chips - d, chips) * 2 + which

    barrier = pltpu.get_barrier_semaphore()
    for e in range(1, samples):
        pl.semaphore_signal(
            barrier, inc=1, device_id={"sample": lax.rem(me + e, samples)}, device_id_type=MESH
        )

    @pl.when(site > 0)
    def _():
        pl.semaphore_signal(barrier, inc=1, device_id={"site": site - 1}, device_id_type=MESH)

    @pl.when(site < sites - 1)
    def _():
        pl.semaphore_signal(barrier, inc=1, device_id={"site": site + 1}, device_id_type=MESH)

    ends = jnp.where(site > 0, 1, 0) + jnp.where(site < sites - 1, 1, 0)
    pl.semaphore_wait(barrier, samples - 1 + ends)

    def remote(src, dst, sent, got, target):
        return pltpu.make_async_remote_copy(
            src_ref=src, dst_ref=dst, send_sem=sent, recv_sem=got,
            device_id=target, device_id_type=MESH,
        )

    def by_rows(owner, b, to):
        return full.at[:, b, pl.ds(pl.multiple_of(owner * micro, SUB), micro), :]

    def by_columns(owner, b, to):
        return full.at[owner, b]

    def by_chip(owner, b, to):
        return full.at[owner, b, pl.ds(pl.multiple_of(to * pair, SUB), pair), :]

    def each(act):
        @pl.when(site == 0)
        def _():
            act(by_rows)

        @pl.when((site > 0) & (site < tail))
        def _():
            act(by_columns)

        @pl.when(is_tail)
        def _():
            act(by_chip)

    def x_copy(block, owner, d, b, to):
        part = block(owner, b, to)
        return remote(
            part, part, x_send.at[d - 1, b], x_recv.at[d - 1, b], {"sample": ahead(d)}
        )

    def s_copy(block, owner, d, b):
        part = block(owner, b, chip)
        return remote(part, part, s_send.at[d, b], s_recv.at[d, b], {"sample": sibling})

    def w_copy(d, c):
        span = pl.ds(c * depth, depth)
        return remote(
            merged.at[span, :], landed.at[d - 1, span, :],
            w_send.at[d - 1, c], w_recv.at[d - 1, c], {"sample": ahead(d)},
        )

    def t_rows(d, b, which):
        at = pl.multiple_of(d * pair + which * micro, SUB)
        return pl.ds(at, micro)

    def t_copy(d, b):
        return remote(
            ybuf.at[b, t_rows(d, b, 1 - core), :], gath.at[behind(d, core), b],
            a_send.at[d, b], a_recv.at[d, b], {"sample": sibling},
        )

    def t_arrival(d, b):
        slot = gath.at[behind(d, 1 - core), b]
        return remote(slot, slot, a_send.at[d, b], a_recv.at[d, b], {"sample": sibling})

    def z_copy(b):
        return remote(
            ybuf.at[b], full.at[me, b], z_send.at[b], z_recv.at[b],
            {"site": jnp.minimum(site + 1, sites - 1)},
        )

    def b_copy(d, b):
        there = pl.ds(behind(d, 0), 2)
        return remote(
            full.at[there, b, pl.ds(pl.multiple_of(me * micro, SUB), micro), :],
            gath.at[there, b], b_send.at[d - 1, b], b_recv.at[d - 1, b],
            {"site": jnp.maximum(site - 1, 0)},
        )

    def u_copy(b):
        return remote(
            ybuf.at[b, pl.ds(pl.multiple_of(sibling * micro, SUB), micro), :],
            gath.at[me, b], a_send.at[0, b], a_recv.at[0, b], {"sample": sibling},
        )

    def u_arrival(b):
        slot = gath.at[sibling, b]
        return remote(slot, slot, a_send.at[0, b], a_recv.at[0, b], {"sample": sibling})

    def p_copy(e):
        target = lax.rem(me + e, samples)
        return remote(
            marks.at[me], marks.at[me], p_send.at[e - 1], p_recv.at[e - 1], {"sample": target}
        )

    def p_arrival(e):
        source = lax.rem(me + samples - e, samples)
        return remote(
            marks.at[source], marks.at[source],
            p_send.at[e - 1], p_recv.at[e - 1], {"sample": source},
        )

    def launch(b):
        def act(block):
            for d in range(1, chips):
                x_copy(block, me, d, b, lax.rem(chip + d, chips)).start()
            s_copy(block, me, 0, b).start()

        each(act)

    marks[me] = jnp.broadcast_to(picks_ref[...].astype(jnp.float32), (8, rows))
    for e in range(1, samples):
        p_copy(e).start()

    @pl.when(site == 0)
    def _():
        for b in range(steps):
            for o in range(samples):
                full[o, b, pl.ds(pl.multiple_of(me * micro, SUB), micro), :] = fronts_ref[
                    b * micro : (b + 1) * micro, o * cols : (o + 1) * cols
                ]
        for b in range(min(2, steps)):
            launch(b)

    def expand(owner, load, save, first, last):
        def body(i, carry):
            left = charges_ref[site, i]
            here = cols // BLOCK
            part, inner = i // here, lax.rem(i, here) * BLOCK
            for j in range(cols // BLOCK):
                right = charges_ref[site + 1, owner * (cols // BLOCK) + j]
                allowed = []
                for p in range(PHYS):
                    fits = jnp.where(right == lax.rem(left + p, CHARGES), 1.0, 0.0)
                    allowed.append(jnp.full((SUB, BLOCK), fits, jnp.float32).astype(jnp.bfloat16))
                lanes = slice(j * BLOCK, (j + 1) * BLOCK)
                for u in range(BLOCK // SUB):
                    at = pl.multiple_of(i * BLOCK + u * SUB, SUB)
                    to = (part, pl.multiple_of(inner + u * SUB, SUB))
                    save(to, at, lanes, [load(p, at, lanes) * allowed[p] for p in range(PHYS)])
            return carry

        lax.fori_loop(first, last, body, 0)

    def load_own(p, at, lanes):
        return tensor_ref[p, pl.ds(at, SUB), lanes]

    def save_own(to, at, lanes, values):
        for p in range(PHYS):
            wf[to[0], pl.ds(p * cols + to[1], SUB), lanes] = values[p]

    def save_tail(to, at, lanes, values):
        save_own(to, at, lanes, values)
        merged[pl.ds(at, SUB), lanes] = values[0] + values[1]

    per = depth // BLOCK

    @pl.when(is_body)
    def _():
        expand(me, load_own, save_own, 0, bond // BLOCK)

    @pl.when(is_tail)
    def _():
        for c in range(pieces):
            expand(me, load_own, save_tail, c * per, (c + 1) * per)
            for d in range(1, chips):
                w_copy(d, c).start()

    for e in range(1, samples):
        p_arrival(e).wait_recv()
    for o in range(samples):
        for j in range(rows // LANES):
            line = marks[o, 0:1, j * LANES : (j + 1) * LANES]
            square = jnp.broadcast_to(line, (LANES, LANES)).T.astype(jnp.bfloat16)
            for q in range(LANES // SUB):
                b, at = divmod(j * LANES + q * SUB, micro)
                columns[b, o * micro + at : o * micro + at + SUB, :] = square[
                    q * SUB : (q + 1) * SUB, :
                ]

    @pl.when(is_tail)
    def _():
        for c in range(pieces):
            for d in range(1, chips):
                w_copy(d, c).wait_recv()

                def load_far(p, at, lanes):
                    return landed[d - 1, pl.ds(at, SUB), lanes]

                def save_far(to, at, lanes, values):
                    for p in range(PHYS):
                        wx[d - 1, to[0], pl.ds(p * cols + to[1], SUB), lanes] = values[p]

                expand(behind(d, core), load_far, save_far, c * per, (c + 1) * per)

    @pl.when(site > 0)
    def _():
        z_copy(0).wait_recv()
        launch(0)

    def forward(b):
        for d in range(1, chips):
            x_copy(by_rows, behind(d, core), d, b, chip).wait_recv()
            s_copy(by_rows, behind(d, core), d, b).start()

    @pl.when(site == 0)
    def _():
        forward(0)

    chip_rows = pl.ds(pl.multiple_of(chip * pair, SUB), pair)

    def contract(b, c, start, last, norms=True):
        if last:
            front, picks, count = full[c, b, chip_rows, :], columns[b, chip_rows, :], pair
        else:
            front, picks, count = full[c, b], columns[b], samples * micro
        second = front * jnp.concatenate([picks] * (cols // LANES), axis=1)
        both = jnp.concatenate([front - second, second], axis=1)
        if norms:
            total = jnp.zeros((count, LANES), jnp.float32)
            for k in range(cols // LANES):
                wide = front[:, k * LANES : (k + 1) * LANES].astype(jnp.float32)
                total = total + wide * wide
            sums[0:count, :] = total if start else sums[0:count, :] + total
        for d in range(chips if last else 1):
            right = wf[c] if d == 0 else wx[d - 1, c]
            part = jnp.dot(both, right, preferred_element_type=jnp.float32)
            acc[d, 0:count, :] = part if start else acc[d, 0:count, :] + part

    def scale_of(count):
        mean = jnp.sum(sums[0:count, :], axis=1, keepdims=True) * (1.0 / bond)
        return 1.0 / jnp.sqrt(mean + epsilon)

    def finish(b):
        total = jnp.zeros((micro, LANES), jnp.float32)
        for c in range(samples):
            for k in range(cols // LANES):
                wide = gath[c, b, :, k * LANES : (k + 1) * LANES].astype(jnp.float32)
                total = total + wide * wide
        norm = jnp.sqrt(jnp.sum(total, axis=1, keepdims=True) * (1.0 / bond) + epsilon)
        inverse = 1.0 / norm
        span = pl.ds(pl.multiple_of(b * micro, SUB), micro)
        logs[span, :] = jnp.broadcast_to(jnp.log(norm), (micro, LANES))
        for c in range(samples):
            wide = gath[c, b].astype(jnp.float32)
            out_ref[span, c * cols : (c + 1) * cols] = (wide * inverse).astype(jnp.bfloat16)

    def finish_body(b, carry):
        gath[me, b] = ybuf[b, pl.ds(pl.multiple_of(me * micro, SUB), micro), :]
        u_arrival(b).wait_recv()
        for d in range(1, chips):
            b_copy(d, b).wait_recv()
        finish(b)
        return carry

    def finish_tail(b):
        for d in range(chips):
            t_arrival(d, b).wait_recv()
        finish(b)

    def early(b, block, last):
        contract(b, me, True, last)
        s_copy(block, sibling, 0, b).wait_recv()
        contract(b, sibling, False, last)

    def late(b, block, last):
        for d in range(1, chips):
            x_copy(block, behind(d, core), d, b, chip).wait_recv()
            s_copy(block, behind(d, core), d, b).start()
            contract(b, behind(d, core), False, last)
            s_copy(block, behind(d, 1 - core), d, b).wait_recv()
            b_copy(d, b).start()
            contract(b, behind(d, 1 - core), False, last)

    def step(b, carry):
        @pl.when((site > 0) & (site < tail))
        def _():
            early(b, by_columns, False)

        @pl.when(is_tail)
        def _():
            early(b, by_chip, True)

        @pl.when((site > 0) & (b + 1 < steps))
        def _():
            z_copy(b + 1).wait_recv()
            launch(b + 1)

        @pl.when((site == 0) & (b + 2 < steps))
        def _():
            launch(b + 2)

        @pl.when(site == 0)
        def _():
            for d in range(chips):
                s_copy(by_rows, behind(d, 1 - core), d, b).wait_recv()
            for c in range(samples - 1):
                contract(b, c, c == 0, False, False)

            @pl.when(b + 1 < steps)
            def _():
                forward(b + 1)

            contract(b, samples - 1, False, False, False)
            ybuf[b] = acc[0].astype(jnp.bfloat16)
            z_copy(b).start()
            u_copy(b).start()

        @pl.when((site > 0) & (site < tail))
        def _():
            late(b, by_columns, False)

        @pl.when(is_tail)
        def _():
            late(b, by_chip, True)

        @pl.when((site > 0) & (site < tail))
        def _():
            ybuf[b] = (acc[0] * scale_of(samples * micro)).astype(jnp.bfloat16)
            z_copy(b).start()
            u_copy(b).start()

        @pl.when(is_tail)
        def _():
            scale = scale_of(pair)
            for d in range(chips):
                ybuf[b, d * pair : (d + 1) * pair, :] = (acc[d, 0:pair, :] * scale).astype(
                    jnp.bfloat16
                )
                t_copy(d, b).start()
                gath[behind(d, core), b] = ybuf[b, t_rows(d, b, core), :]

        @pl.when(is_tail & (b > 0))
        def _():
            finish_tail(b - 1)

        return carry

    lax.fori_loop(0, steps, step, 0)

    @pl.when(is_tail)
    def _():
        finish_tail(steps - 1)

    @pl.when(is_body)
    def _():
        lax.fori_loop(0, steps, finish_body, 0)

    for j in range(rows // LANES):
        square = logs[j * LANES : (j + 1) * LANES, :].T
        log_ref[0:1, j * LANES : (j + 1) * LANES] = square[0:1, :]

    for e in range(1, samples):
        p_copy(e).wait_send()

    @pl.when(is_tail)
    def _():
        for c in range(pieces):
            for d in range(1, chips):
                w_copy(d, c).wait_send()

    def drain(b, carry):
        def act(block):
            for d in range(1, chips):
                x_copy(block, me, d, b, lax.rem(chip + d, chips)).wait_send()
            for d in range(chips):
                s_copy(block, behind(d, core), d, b).wait_send()

        each(act)

        @pl.when(site > 0)
        def _():
            for d in range(1, chips):
                b_copy(d, b).wait_send()

        @pl.when(is_body)
        def _():
            u_copy(b).wait_send()

        @pl.when(is_tail)
        def _():
            for d in range(chips):
                t_copy(d, b).wait_send()

        @pl.when(site < sites - 1)
        def _():
            z_copy(b).wait_send()

        return carry

    lax.fori_loop(0, steps, drain, 0)


def micro_rows(rows):
    best = rows
    for count in range(1, rows // SUB + 1):
        if rows % count == 0 and (rows // count) % SUB == 0:
            best = rows // count
            if count >= 8:
                break
    return best


def per_device(site_tensor, fronts_in, outcomes, charges):
    sites = lax.axis_size("site")
    samples = lax.axis_size("sample")
    chips = samples // 2
    _, bond, _, cols = site_tensor.shape
    rows = fronts_in.shape[0]
    tensor = site_tensor[0].transpose(1, 0, 2)
    pieces = 4

    micro = micro_rows(rows)
    steps = rows // micro
    vmem = pl.BlockSpec(memory_space=pltpu.VMEM)
    dma = pltpu.SemaphoreType.DMA
    peers = max(chips - 1, 1)
    fronts, logs = pl.pallas_call(
        functools.partial(chain_kernel, chips, sites, micro, pieces),
        out_shape=(
            jax.ShapeDtypeStruct((rows, bond), jnp.bfloat16),
            jax.ShapeDtypeStruct((1, rows), jnp.float32),
        ),
        in_specs=[vmem, pl.BlockSpec(memory_space=pltpu.SMEM), vmem, vmem],
        out_specs=(vmem, vmem),
        scratch_shapes=[
            pltpu.VMEM((samples, PHYS * cols, cols), jnp.bfloat16),
            pltpu.VMEM((peers, samples, PHYS * cols, cols), jnp.bfloat16),
            pltpu.VMEM((bond, cols), jnp.bfloat16),
            pltpu.VMEM((peers, bond, cols), jnp.bfloat16),
            pltpu.VMEM((samples, steps, samples * micro, cols), jnp.bfloat16),
            pltpu.VMEM((chips, samples * micro, cols), jnp.float32),
            pltpu.VMEM((samples * micro, LANES), jnp.float32),
            pltpu.VMEM((steps, samples * micro, cols), jnp.bfloat16),
            pltpu.VMEM((samples, steps, micro, cols), jnp.bfloat16),
            pltpu.VMEM((samples, 8, rows), jnp.float32),
            pltpu.VMEM((steps, samples * micro, LANES), jnp.bfloat16),
            pltpu.VMEM((rows, LANES), jnp.float32),
            dma((peers, steps)),
            dma((peers, steps)),
            dma((chips, steps)),
            dma((chips, steps)),
            dma((steps,)),
            dma((steps,)),
            dma((chips, steps)),
            dma((chips, steps)),
            dma((samples - 1,)),
            dma((samples - 1,)),
            dma((peers, pieces)),
            dma((peers, pieces)),
            dma((peers, steps)),
            dma((peers, steps)),
        ],
        compiler_params=pltpu.CompilerParams(
            collective_id=0, has_side_effects=True, vmem_limit_bytes=36 * 2**20
        ),
        cost_estimate=pl.CostEstimate(
            flops=4 * rows * bond * bond, bytes_accessed=8 * bond * bond, transcendentals=rows
        ),
    )(tensor, charges, fronts_in, outcomes)
    return fronts[None], logs


def solution(mesh):
    in_specs = (
        P(("groups", "site"), None, None, "sample"),
        P(("groups", "sample"), None),
        P(("groups", "site"), "sample"),
        P("groups", None),
    )
    out_specs = (P(("groups", "site"), "sample", None), P(("groups", "site"), "sample"))
    return jax.shard_map(
        per_device, mesh=mesh, in_specs=in_specs, out_specs=out_specs, check_vma=False
    )
```

```python
import functools

import jax
import jax.numpy as jnp
from jax import lax
from jax.experimental import pallas as pl
from jax.experimental.pallas import tpu as pltpu
from jax.sharding import PartitionSpec as P

BLOCK = 128
CHARGES = 4
PHYS = 2
LANES = 128
SUB = 16
MESH = pl.DeviceIdType.MESH

epsilon = 1e-06


def chain_kernel(
    chips, sites, micro, pieces, tensor_ref, charges_ref, fronts_ref, picks_ref,
    out_ref, log_ref,
    wf, wx, merged, landed, full, acc, sums, ybuf, gath, marks, columns, logs,
    x_send, x_recv, s_send, s_recv, z_send, z_recv, a_send, a_recv, p_send, p_recv,
    w_send, w_recv, b_send, b_recv,
):
    samples = 2 * chips
    site = lax.axis_index("site")
    me = lax.axis_index("sample")
    chip, core = me // 2, lax.rem(me, 2)
    sibling = chip * 2 + (1 - core)
    _, bond, cols = tensor_ref.shape
    rows = fronts_ref.shape[0]
    steps = rows // micro
    pair = 2 * micro
    depth = bond // pieces
    tail = sites - 1
    is_tail, is_body = site == tail, site != tail

    def ahead(d):
        return lax.rem(chip + d, chips) * 2 + core

    def behind(d, which):
        return lax.rem(chip + chips - d, chips) * 2 + which

    barrier = pltpu.get_barrier_semaphore()
    for e in range(1, samples):
        pl.semaphore_signal(
            barrier, inc=1, device_id={"sample": lax.rem(me + e, samples)}, device_id_type=MESH
        )

    @pl.when(site > 0)
    def _():
        pl.semaphore_signal(barrier, inc=1, device_id={"site": site - 1}, device_id_type=MESH)

    @pl.when(site < sites - 1)
    def _():
        pl.semaphore_signal(barrier, inc=1, device_id={"site": site + 1}, device_id_type=MESH)

    ends = jnp.where(site > 0, 1, 0) + jnp.where(site < sites - 1, 1, 0)
    pl.semaphore_wait(barrier, samples - 1 + ends)

    def remote(src, dst, sent, got, target):
        return pltpu.make_async_remote_copy(
            src_ref=src, dst_ref=dst, send_sem=sent, recv_sem=got,
            device_id=target, device_id_type=MESH,
        )

    def by_rows(owner, b, to):
        return full.at[:, b, pl.ds(pl.multiple_of(owner * micro, SUB), micro), :]

    def by_columns(owner, b, to):
        return full.at[owner, b]

    def by_chip(owner, b, to):
        return full.at[owner, b, pl.ds(pl.multiple_of(to * pair, SUB), pair), :]

    def each(act):
        @pl.when(site == 0)
        def _():
            act(by_rows)

        @pl.when((site > 0) & (site < tail))
        def _():
            act(by_columns)

        @pl.when(is_tail)
        def _():
            act(by_chip)

    def x_copy(block, owner, d, b, to):
        part = block(owner, b, to)
        return remote(
            part, part, x_send.at[d - 1, b], x_recv.at[d - 1, b], {"sample": ahead(d)}
        )

    def s_copy(block, owner, d, b):
        part = block(owner, b, chip)
        return remote(part, part, s_send.at[d, b], s_recv.at[d, b], {"sample": sibling})

    def w_copy(d, c):
        span = pl.ds(c * depth, depth)
        return remote(
            merged.at[span, :], landed.at[d - 1, span, :],
            w_send.at[d - 1, c], w_recv.at[d - 1, c], {"sample": ahead(d)},
        )

    def t_rows(d, b, which):
        at = pl.multiple_of(d * pair + which * micro, SUB)
        return pl.ds(at, micro)

    def t_copy(d, b):
        return remote(
            ybuf.at[b, t_rows(d, b, 1 - core), :], gath.at[behind(d, core), b],
            a_send.at[d, b], a_recv.at[d, b], {"sample": sibling},
        )

    def t_arrival(d, b):
        slot = gath.at[behind(d, 1 - core), b]
        return remote(slot, slot, a_send.at[d, b], a_recv.at[d, b], {"sample": sibling})

    def z_copy(b):
        return remote(
            ybuf.at[b], full.at[me, b], z_send.at[b], z_recv.at[b],
            {"site": jnp.minimum(site + 1, sites - 1)},
        )

    def b_copy(d, b):
        there = pl.ds(behind(d, 0), 2)
        return remote(
            full.at[there, b, pl.ds(pl.multiple_of(me * micro, SUB), micro), :],
            gath.at[there, b], b_send.at[d - 1, b], b_recv.at[d - 1, b],
            {"site": jnp.maximum(site - 1, 0)},
        )

    def u_copy(b):
        return remote(
            ybuf.at[b, pl.ds(pl.multiple_of(sibling * micro, SUB), micro), :],
            gath.at[me, b], a_send.at[0, b], a_recv.at[0, b], {"sample": sibling},
        )

    def u_arrival(b):
        slot = gath.at[sibling, b]
        return remote(slot, slot, a_send.at[0, b], a_recv.at[0, b], {"sample": sibling})

    def p_copy(e):
        target = lax.rem(me + e, samples)
        return remote(
            marks.at[me], marks.at[me], p_send.at[e - 1], p_recv.at[e - 1], {"sample": target}
        )

    def p_arrival(e):
        source = lax.rem(me + samples - e, samples)
        return remote(
            marks.at[source], marks.at[source],
            p_send.at[e - 1], p_recv.at[e - 1], {"sample": source},
        )

    def launch(b):
        def act(block):
            for d in range(1, chips):
                x_copy(block, me, d, b, lax.rem(chip + d, chips)).start()
            s_copy(block, me, 0, b).start()

        each(act)

    @pl.when(site == 0)
    def _():
        for b in range(steps):
            for o in range(samples):
                full[o, b, pl.ds(pl.multiple_of(me * micro, SUB), micro), :] = fronts_ref[
                    b * micro : (b + 1) * micro, o * cols : (o + 1) * cols
                ]
            if b < 2:
                launch(b)

    marks[me] = jnp.broadcast_to(picks_ref[...].astype(jnp.float32), (8, rows))
    for e in range(1, samples):
        p_copy(e).start()

    def expand(owner, load, save, first, last):
        def body(i, carry):
            left = charges_ref[site, i]
            here = cols // BLOCK
            part, inner = i // here, lax.rem(i, here) * BLOCK
            for j in range(cols // BLOCK):
                right = charges_ref[site + 1, owner * (cols // BLOCK) + j]
                allowed = []
                for p in range(PHYS):
                    fits = jnp.where(right == lax.rem(left + p, CHARGES), 1.0, 0.0)
                    allowed.append(jnp.full((SUB, BLOCK), fits, jnp.float32).astype(jnp.bfloat16))
                lanes = slice(j * BLOCK, (j + 1) * BLOCK)
                for u in range(BLOCK // SUB):
                    at = pl.multiple_of(i * BLOCK + u * SUB, SUB)
                    to = (part, pl.multiple_of(inner + u * SUB, SUB))
                    save(to, at, lanes, [load(p, at, lanes) * allowed[p] for p in range(PHYS)])
            return carry

        lax.fori_loop(first, last, body, 0)

    def load_own(p, at, lanes):
        return tensor_ref[p, pl.ds(at, SUB), lanes]

    def save_own(to, at, lanes, values):
        for p in range(PHYS):
            wf[to[0], pl.ds(p * cols + to[1], SUB), lanes] = values[p]

    def save_tail(to, at, lanes, values):
        save_own(to, at, lanes, values)
        merged[pl.ds(at, SUB), lanes] = values[0] + values[1]

    per = depth // BLOCK

    @pl.when(is_body)
    def _():
        expand(me, load_own, save_own, 0, bond // BLOCK)

    @pl.when(is_tail)
    def _():
        for c in range(pieces):
            expand(me, load_own, save_tail, c * per, (c + 1) * per)
            for d in range(1, chips):
                w_copy(d, c).start()

    for e in range(1, samples):
        p_arrival(e).wait_recv()
    for o in range(samples):
        for j in range(rows // LANES):
            line = marks[o, 0:1, j * LANES : (j + 1) * LANES]
            square = jnp.broadcast_to(line, (LANES, LANES)).T.astype(jnp.bfloat16)
            for q in range(LANES // SUB):
                b, at = divmod(j * LANES + q * SUB, micro)
                columns[b, o * micro + at : o * micro + at + SUB, :] = square[
                    q * SUB : (q + 1) * SUB, :
                ]

    @pl.when(is_tail)
    def _():
        for c in range(pieces):
            for d in range(1, chips):
                w_copy(d, c).wait_recv()

                def load_far(p, at, lanes):
                    return landed[d - 1, pl.ds(at, SUB), lanes]

                def save_far(to, at, lanes, values):
                    for p in range(PHYS):
                        wx[d - 1, to[0], pl.ds(p * cols + to[1], SUB), lanes] = values[p]

                expand(behind(d, core), load_far, save_far, c * per, (c + 1) * per)

    @pl.when(site > 0)
    def _():
        z_copy(0).wait_recv()
        launch(0)

    def forward(b):
        for d in range(1, chips):
            x_copy(by_rows, behind(d, core), d, b, chip).wait_recv()
            s_copy(by_rows, behind(d, core), d, b).start()

    @pl.when(site == 0)
    def _():
        forward(0)

    chip_rows = pl.ds(pl.multiple_of(chip * pair, SUB), pair)

    def contract(b, c, start, last, norms=True):
        if last:
            front, picks, count = full[c, b, chip_rows, :], columns[b, chip_rows, :], pair
        else:
            front, picks, count = full[c, b], columns[b], samples * micro
        second = front * jnp.concatenate([picks] * (cols // LANES), axis=1)
        both = jnp.concatenate([front - second, second], axis=1)
        if norms:
            total = jnp.zeros((count, LANES), jnp.float32)
            for k in range(cols // LANES):
                wide = front[:, k * LANES : (k + 1) * LANES].astype(jnp.float32)
                total = total + wide * wide
            sums[0:count, :] = total if start else sums[0:count, :] + total
        for d in range(chips if last else 1):
            right = wf[c] if d == 0 else wx[d - 1, c]
            part = jnp.dot(both, right, preferred_element_type=jnp.float32)
            acc[d, 0:count, :] = part if start else acc[d, 0:count, :] + part

    def scale_of(count):
        mean = jnp.sum(sums[0:count, :], axis=1, keepdims=True) * (1.0 / bond)
        return 1.0 / jnp.sqrt(mean + epsilon)

    def finish(b):
        total = jnp.zeros((micro, LANES), jnp.float32)
        for c in range(samples):
            for k in range(cols // LANES):
                wide = gath[c, b, :, k * LANES : (k + 1) * LANES].astype(jnp.float32)
                total = total + wide * wide
        norm = jnp.sqrt(jnp.sum(total, axis=1, keepdims=True) * (1.0 / bond) + epsilon)
        inverse = 1.0 / norm
        span = pl.ds(pl.multiple_of(b * micro, SUB), micro)
        logs[span, :] = jnp.broadcast_to(jnp.log(norm), (micro, LANES))
        for c in range(samples):
            wide = gath[c, b].astype(jnp.float32)
            out_ref[span, c * cols : (c + 1) * cols] = (wide * inverse).astype(jnp.bfloat16)

    def finish_body(b, carry):
        gath[me, b] = ybuf[b, pl.ds(pl.multiple_of(me * micro, SUB), micro), :]
        u_arrival(b).wait_recv()
        for d in range(1, chips):
            b_copy(d, b).wait_recv()
        finish(b)
        return carry

    def finish_tail(b):
        for d in range(chips):
            t_arrival(d, b).wait_recv()
        finish(b)

    def early(b, block, last):
        contract(b, me, True, last)
        s_copy(block, sibling, 0, b).wait_recv()
        contract(b, sibling, False, last)

    def late(b, block, last):
        for d in range(1, chips):
            x_copy(block, behind(d, core), d, b, chip).wait_recv()
            s_copy(block, behind(d, core), d, b).start()
            contract(b, behind(d, core), False, last)
            s_copy(block, behind(d, 1 - core), d, b).wait_recv()
            b_copy(d, b).start()
            contract(b, behind(d, 1 - core), False, last)

    def step(b, carry):
        @pl.when((site > 0) & (site < tail))
        def _():
            early(b, by_columns, False)

        @pl.when(is_tail)
        def _():
            early(b, by_chip, True)

        @pl.when((site > 0) & (b + 1 < steps))
        def _():
            z_copy(b + 1).wait_recv()
            launch(b + 1)

        @pl.when((site == 0) & (b + 2 < steps))
        def _():
            launch(b + 2)

        @pl.when(site == 0)
        def _():
            for d in range(chips):
                s_copy(by_rows, behind(d, 1 - core), d, b).wait_recv()
            for c in range(samples - 1):
                contract(b, c, c == 0, False, False)

            @pl.when(b + 1 < steps)
            def _():
                forward(b + 1)

            contract(b, samples - 1, False, False, False)
            ybuf[b] = acc[0].astype(jnp.bfloat16)
            z_copy(b).start()
            u_copy(b).start()

        @pl.when((site > 0) & (site < tail))
        def _():
            late(b, by_columns, False)

        @pl.when(is_tail)
        def _():
            late(b, by_chip, True)

        @pl.when((site > 0) & (site < tail))
        def _():
            ybuf[b] = (acc[0] * scale_of(samples * micro)).astype(jnp.bfloat16)
            z_copy(b).start()
            u_copy(b).start()

        @pl.when(is_tail)
        def _():
            scale = scale_of(pair)
            for d in range(chips):
                ybuf[b, d * pair : (d + 1) * pair, :] = (acc[d, 0:pair, :] * scale).astype(
                    jnp.bfloat16
                )
                t_copy(d, b).start()
                gath[behind(d, core), b] = ybuf[b, t_rows(d, b, core), :]

        @pl.when(is_tail & (b > 0))
        def _():
            finish_tail(b - 1)

        return carry

    lax.fori_loop(0, steps, step, 0)

    @pl.when(is_tail)
    def _():
        finish_tail(steps - 1)

    @pl.when(is_body)
    def _():
        lax.fori_loop(0, steps, finish_body, 0)

    for j in range(rows // LANES):
        square = logs[j * LANES : (j + 1) * LANES, :].T
        log_ref[0:1, j * LANES : (j + 1) * LANES] = square[0:1, :]

    for e in range(1, samples):
        p_copy(e).wait_send()

    @pl.when(is_tail)
    def _():
        for c in range(pieces):
            for d in range(1, chips):
                w_copy(d, c).wait_send()

    def drain(b, carry):
        def act(block):
            for d in range(1, chips):
                x_copy(block, me, d, b, lax.rem(chip + d, chips)).wait_send()
            for d in range(chips):
                s_copy(block, behind(d, core), d, b).wait_send()

        each(act)

        @pl.when(site > 0)
        def _():
            for d in range(1, chips):
                b_copy(d, b).wait_send()

        @pl.when(is_body)
        def _():
            u_copy(b).wait_send()

        @pl.when(is_tail)
        def _():
            for d in range(chips):
                t_copy(d, b).wait_send()

        @pl.when(site < sites - 1)
        def _():
            z_copy(b).wait_send()

        return carry

    lax.fori_loop(0, steps, drain, 0)


def micro_rows(rows):
    best = rows
    for count in range(1, rows // SUB + 1):
        if rows % count == 0 and (rows // count) % SUB == 0:
            best = rows // count
            if count >= 8:
                break
    return best


def per_device(site_tensor, fronts_in, outcomes, charges):
    sites = lax.axis_size("site")
    samples = lax.axis_size("sample")
    chips = samples // 2
    _, bond, _, cols = site_tensor.shape
    rows = fronts_in.shape[0]
    tensor = site_tensor[0].transpose(1, 0, 2)
    pieces = 4

    micro = micro_rows(rows)
    steps = rows // micro
    vmem = pl.BlockSpec(memory_space=pltpu.VMEM)
    dma = pltpu.SemaphoreType.DMA
    peers = max(chips - 1, 1)
    fronts, logs = pl.pallas_call(
        functools.partial(chain_kernel, chips, sites, micro, pieces),
        out_shape=(
            jax.ShapeDtypeStruct((rows, bond), jnp.bfloat16),
            jax.ShapeDtypeStruct((1, rows), jnp.float32),
        ),
        in_specs=[vmem, pl.BlockSpec(memory_space=pltpu.SMEM), vmem, vmem],
        out_specs=(vmem, vmem),
        scratch_shapes=[
            pltpu.VMEM((samples, PHYS * cols, cols), jnp.bfloat16),
            pltpu.VMEM((peers, samples, PHYS * cols, cols), jnp.bfloat16),
            pltpu.VMEM((bond, cols), jnp.bfloat16),
            pltpu.VMEM((peers, bond, cols), jnp.bfloat16),
            pltpu.VMEM((samples, steps, samples * micro, cols), jnp.bfloat16),
            pltpu.VMEM((chips, samples * micro, cols), jnp.float32),
            pltpu.VMEM((samples * micro, LANES), jnp.float32),
            pltpu.VMEM((steps, samples * micro, cols), jnp.bfloat16),
            pltpu.VMEM((samples, steps, micro, cols), jnp.bfloat16),
            pltpu.VMEM((samples, 8, rows), jnp.float32),
            pltpu.VMEM((steps, samples * micro, LANES), jnp.bfloat16),
            pltpu.VMEM((rows, LANES), jnp.float32),
            dma((peers, steps)),
            dma((peers, steps)),
            dma((chips, steps)),
            dma((chips, steps)),
            dma((steps,)),
            dma((steps,)),
            dma((chips, steps)),
            dma((chips, steps)),
            dma((samples - 1,)),
            dma((samples - 1,)),
            dma((peers, pieces)),
            dma((peers, pieces)),
            dma((peers, steps)),
            dma((peers, steps)),
        ],
        compiler_params=pltpu.CompilerParams(
            collective_id=0, has_side_effects=True, vmem_limit_bytes=36 * 2**20
        ),
        cost_estimate=pl.CostEstimate(
            flops=4 * rows * bond * bond, bytes_accessed=8 * bond * bond, transcendentals=rows
        ),
    )(tensor, charges, fronts_in, outcomes)
    return fronts[None], logs


def solution(mesh):
    in_specs = (
        P(("groups", "site"), None, None, "sample"),
        P(("groups", "sample"), None),
        P(("groups", "site"), "sample"),
        P("groups", None),
    )
    out_specs = (P(("groups", "site"), "sample", None), P(("groups", "site"), "sample"))
    return jax.shard_map(
        per_device, mesh=mesh, in_specs=in_specs, out_specs=out_specs, check_vma=False
    )
```
